32 devices in a mesh: view: 4 (over z), space: 8 (over y, x, core).
Axes of the slice: x: 2, y: 2, z: 4, core: 2. Of those that a mesh axis runs over, the one named last changes fastest.
Arguments:
- prior: float32 [128, 64, 256], P('space'), may hold values from 0.5 to 2
- data: float32 [8, 128, 64, 256], P('view', 'space'), may hold values from 0.1 to 10
- taps: float32 [8, 3, 32], P('view'), may hold values from 0.03 to 8.3
- offsets: int32 [8], P('view'), may hold values from 0 to 7
- coverage: int32 [8, 128], P('view', 'space'), may hold values from 0 to 1, as said below
Outputs:
- estimate: float32 [128, 64, 256], P('space')
The draws below stay inside these ranges and needn't reach their ends.
Inputs may be any that keep to these rules, and one draw needn't show every extreme that they name: `coverage`: every plane of the first dimension is covered by at least one view.
All inputs are finite; a program needn't handle non-finite values.
Results may differ from the reference program's by a relative error of at most 0.000098.
Values sent between devices are 32-bit elements; how exact they have to be, the bound alone decides.
No kernel may reach another device: no remote copies, remote signals or barrier semaphores. Data moves between devices by JAX's collectives and lax.ppermute only.
A program may use at most 64 MiB of HBM per device.

```python
import math
import jax
import jax.numpy as jnp
from jax import lax

CX = 16
NY = 64
NZ = 256
TAPS = 32
ITERS = 2
VIEWS = 8
NX = 128
N_SPACE = 8


def draw_coverage(key, part):
    key = jax.random.fold_in(key, 11)
    first, second, third = jax.random.split(key, 3)
    start = jax.random.randint(first, (VIEWS, 1), 0, NX)
    length = jax.random.randint(second, (VIEWS, 1), NX // 4, NX + 1)
    planes = jnp.arange(NX)[None, :]
    inside = (planes - start) % NX < length
    full = jax.random.randint(third, (), 0, VIEWS)
    cover = inside | (jnp.arange(VIEWS)[:, None] == full)
    return cover.astype(jnp.int32)


def draw_data(key, part):
    key = jax.random.fold_in(key, 23)
    first, second = jax.random.split(key)
    speckle = jax.random.uniform(first, (VIEWS, NX, NY, NZ), jnp.float32, -0.9, 0.9)
    shading = jax.random.uniform(second, (VIEWS, 1, NY // 2, NZ // 2), jnp.float32, -1.3, 1.3)
    shading = jnp.repeat(jnp.repeat(shading, 2, axis=2), 2, axis=3)
    return jnp.clip(jnp.exp(speckle + shading), 0.1, 10.0)


def draw_taps(key, part):
    key = jax.random.fold_in(key, 37)
    first, second, third, fourth = jax.random.split(key, 4)
    tail_taps = jnp.exp(jax.random.uniform(first, (VIEWS, 3, TAPS), jnp.float32, jnp.log(0.03), jnp.log(0.3)))
    spread = jnp.exp(jax.random.uniform(second, (VIEWS, 3, 1), jnp.float32, jnp.log(0.5), jnp.log(2.0)))
    height = jnp.exp(jax.random.uniform(third, (VIEWS, 3, 1), jnp.float32, jnp.log(2.0), jnp.log(8.0)))
    middle = TAPS // 2 + jax.random.uniform(fourth, (VIEWS, 3, 1), jnp.float32, -1.0, 1.0)
    positions = jnp.arange(TAPS, dtype=jnp.float32)[None, None, :]
    return tail_taps + height * jnp.exp(-0.5 * ((positions - middle) / spread) ** 2)


def plant(values, key, least, top_value):
    index_at = [jax.random.randint(jax.random.fold_in(key, axis), (), 0, length) for axis, length in enumerate(values.shape)]
    main_axis = values.shape.index(max(values.shape))
    neighbour = index_at[:main_axis] + [(index_at[main_axis] + 1) % values.shape[main_axis]] + index_at[main_axis + 1:]
    return values.at[tuple(index_at)].set(least).at[tuple(neighbour)].set(top_value)


def block_levels(rng, extent, cuts, least, largest):
    def one(position, shards_of):
        heights = jax.random.uniform(jax.random.fold_in(jax.random.fold_in(rng, 6), position), (shards_of,), jnp.float32, least / len(cuts), largest / len(cuts))
        return jnp.repeat(jnp.exp(heights), extent[position] // shards_of).reshape((-1,) + (1,) * (len(extent) - position - 1))

    gain = one(*cuts[0])
    for cut in cuts[1:]:
        gain = gain * one(*cut)
    return gain


def setup_inputs(seed: int = 0) -> dict:
    arg_keys = jax.random.split(jax.random.key(seed), 6)
    prior = jnp.clip(jnp.exp(math.log(2.0) - 1.3862944 * jax.random.uniform(arg_keys[0], (NX, NY, NZ), jnp.float32) ** block_levels(arg_keys[0], (NX, NY, NZ), ((0, 8),), -0.2, 0.2)), 0.5, 2.0)
    data = draw_data(jax.random.fold_in(arg_keys[5], 71), 0)
    taps = draw_taps(jax.random.fold_in(arg_keys[5], 71), 0)
    offsets = plant(jax.random.randint(arg_keys[3], (VIEWS,), 0, N_SPACE), jax.random.fold_in(arg_keys[3], 1), 0, N_SPACE - 1).astype(jnp.int32)
    coverage = draw_coverage(jax.random.fold_in(arg_keys[5], 71), 0)
    return {"prior": prior, "data": data, "taps": taps, "offsets": offsets, "coverage": coverage}


def blur_axis(field, kern, axis, flip):
    reach = kern.shape[0] // 2
    size = field.shape[axis]
    pads = [(0, 0), (0, 0), (0, 0)]
    pads[axis] = (reach, reach)
    padded = jnp.pad(field, pads)
    total = jnp.zeros_like(field)
    for tap in range(kern.shape[0]):
        start = 2 * reach - tap if flip else tap
        total = total + kern[tap] * lax.slice_in_dim(padded, start, start + size, axis=axis)
    return total


def reference(prior, data, taps, offsets, coverage):
    kern = taps / jnp.sum(taps, axis=-1, keepdims=True)
    weight = coverage.astype(jnp.float32)
    count = jnp.sum(weight, axis=0)
    blocks = jnp.arange(N_SPACE, dtype=jnp.int32)
    estimate = prior
    for step in range(ITERS):
        total = jnp.zeros_like(prior)
        for view in range(VIEWS):
            order = (blocks + offsets[view]) % N_SPACE
            observed = data[view].reshape((N_SPACE, CX) + prior.shape[1:])[order].reshape(prior.shape)
            blurred = estimate
            for axis in range(3):
                blurred = blur_axis(blurred, kern[view, axis], axis, False)
            ratio = observed / blurred
            back = ratio
            for axis in range(3):
                back = blur_axis(back, kern[view, axis], axis, True)
            total = total + weight[view][:, None, None] * back
        estimate = estimate * total / count[:, None, None]
    return estimate
```

```python
import jax
import jax.numpy as jnp
from jax import lax
from jax.sharding import PartitionSpec as P

ITERS = 2
HIGH = lax.Precision.HIGH


def swap(value, axis, mask):
    count = lax.axis_size(axis)
    return lax.ppermute(value, axis, [(i, i ^ mask) for i in range(count)])


def pick(kern, index):
    hit = index[..., None] == jnp.arange(kern.shape[-1])
    lead = kern.reshape(kern.shape[:1] + (1,) * (index.ndim - 1) + kern.shape[1:])
    return jnp.sum(jnp.where(hit, lead, 0.0), axis=-1)


def pack(edge):
    rows, planes, cells = edge.shape
    group = 128 // cells
    edge = edge.reshape(rows // group, group, planes, cells)
    return edge.transpose(0, 2, 1, 3).reshape(rows // group, planes, 128)


def unpack(packed, cells):
    lead = packed.shape[:-2]
    octets, planes, lanes = packed.shape[-3], packed.shape[-2], packed.shape[-1]
    del octets
    group = lanes // cells
    parts = packed.reshape(packed.shape[:-1] + (group, cells))
    parts = jnp.swapaxes(parts, -3, -2)
    return parts.reshape(lead[:-1] + (lead[-1] * group, planes, cells))


def halve(blocks, mask):
    order = blocks.shape[0]
    split = blocks.reshape((order // (2 * mask), 2, mask) + blocks.shape[1:])
    kept = split[:, 0] + swap(split[:, 1], "space", mask)
    return kept.reshape((order // 2,) + blocks.shape[1:])


def scatter_sum(blocks):
    bits = blocks.shape[0].bit_length() - 1
    blocks = halve(blocks, 1)
    middle = blocks.shape[1] // 2
    shift = (bits - 1) // 2
    out = []
    for part, turned in ((blocks[:, :middle], 0), (blocks[:, middle:], shift)):
        left = list(range(1, bits))
        for bit in [1 + (k + turned) % (bits - 1) for k in range(bits - 1)]:
            at = left.index(bit)
            order = part.shape[0]
            low = 1 << at
            split = part.reshape((order // (2 * low), 2, low) + part.shape[1:])
            part = split[:, 0] + swap(split[:, 1], "space", 1 << bit)
            part = part.reshape((order // 2,) + part.shape[2:])
            left.remove(bit)
        out.append(part[0])
    return jnp.concatenate(out, axis=0)


def body(prior, data, taps, offsets, coverage):
    nview, nspace = lax.axis_size("view"), lax.axis_size("space")
    g, j = lax.axis_index("view"), lax.axis_index("space")
    zh, yh = g >> 1, (g ^ (g >> 1)) & 1
    local, width, ny, nz = data.shape
    ntaps = taps.shape[-1]
    rad = ntaps // 2
    hy, hz = ny // 2, nz // 2
    wy = hy + rad

    def quadrant(owner):
        oz, oy = owner >> 1, (owner ^ (owner >> 1)) & 1
        return lax.dynamic_slice(data, (0, 0, oy * hy, oz * hz), (local, width, hy, hz))

    pieces = [quadrant(g)] + [swap(quadrant(g ^ r), "view", r) for r in range(1, nview)]

    flat = jnp.concatenate(
        [
            taps.reshape(local, -1),
            offsets.astype(jnp.float32)[:, None],
            coverage.astype(jnp.float32),
        ],
        axis=1,
    )
    used = flat.shape[1]
    flat = jnp.pad(flat, ((0, 0), (0, -used % 128)))
    every = lax.all_gather(flat, ("view", "space"))
    every = every.reshape((nview, nspace) + flat.shape)
    every = jnp.concatenate(
        [lax.dynamic_slice_in_dim(every, g ^ r, 1, axis=0) for r in range(nview)], axis=0
    )
    nviews = nview * local
    shared = every[:, 0].reshape(nviews, -1)
    kern = shared[:, : 3 * ntaps].reshape(nviews, 3, ntaps)
    kern = kern / jnp.sum(kern, axis=-1, keepdims=True)
    turn = shared[:, 3 * ntaps].astype(jnp.int32)
    cover = every[..., 3 * ntaps + 1 : used].transpose(0, 2, 1, 3).reshape(nviews, nspace, width)
    count = lax.dynamic_index_in_dim(jnp.sum(cover, axis=0), j, 0, keepdims=False)

    slab = (j - turn) % nspace
    place = slab[:, None] * width + jnp.arange(width)
    planes = jnp.arange(nspace * width).reshape(nspace, width)
    band_x = pick(kern[:, 0], planes - place[:, :, None, None] + rad)
    relative = j ^ jnp.arange(nspace)
    planes_r = relative[:, None] * width + jnp.arange(width)
    band_xt = pick(kern[:, 0], planes_r - place[:, :, None, None] + rad)
    cover_r = jnp.concatenate(
        [lax.dynamic_slice_in_dim(cover, j ^ r, 1, axis=1) for r in range(nspace)], axis=1
    )
    band_xt = band_xt * cover_r[:, None]
    rows = jnp.arange(wy) + rad * yh
    band_y = pick(kern[:, 1], (rows - (jnp.arange(hy)[:, None] + hy * yh) + rad)[None])
    cells = jnp.concatenate([jnp.arange(hz) + hz * zh, jnp.arange(rad) + jnp.where(zh == 0, hz, hz - rad)])
    band_z = pick(kern[:, 2], (cells - (jnp.arange(hz)[:, None] + hz * zh) + rad)[None])

    window = lax.dynamic_slice_in_dim(prior, rad * yh, wy, axis=1).transpose(1, 0, 2)
    main = lax.dynamic_slice_in_dim(window, hz * zh, hz, axis=2)
    rim = lax.dynamic_slice_in_dim(window, jnp.where(zh == 0, hz, hz - rad), rad, axis=2)
    estimate = jnp.concatenate([main, pack(rim)], axis=0)

    observed = jnp.concatenate(pieces, axis=0).transpose(0, 2, 1, 3)

    for step in range(ITERS):
        wide = lax.all_gather(estimate, "space")
        wide = jnp.concatenate([wide[:, :wy], unpack(wide[:, wy:], rad)], axis=-1)
        inner = jnp.einsum("vibx,byxz->vyiz", band_x, wide, precision=HIGH)
        inner = jnp.einsum("vyiz,vwz->vyiw", inner, band_z, precision=HIGH)
        blurred = jnp.einsum("vyiw,voy->voiw", inner, band_y, precision=HIGH)
        ratio = observed / blurred
        inner = jnp.einsum("voiw,voy->vyiw", ratio, band_y, precision=HIGH)
        inner = jnp.einsum("vyiw,vwz->vyiz", inner, band_z, precision=HIGH)
        total = jnp.einsum("vibx,vyiz->byxz", band_xt, inner, precision=HIGH)
        rim = jax.vmap(pack)(total[..., hz:])
        total = jnp.concatenate([total[..., :hz], rim], axis=1)
        total = scatter_sum(total)
        main, rim = total[:wy], unpack(total[wy:], rad)
        start = jnp.where(yh == 0, wy - hy, 0)
        edge = jnp.where(zh == 0, main[..., hz - rad :], main[..., :rad])

        def overlap(value):
            return lax.dynamic_slice_in_dim(value, start, hy, axis=0)

        from_y = swap(jnp.concatenate([overlap(main), pack(overlap(rim))], axis=0), "view", 1)
        from_z = swap(jnp.concatenate([pack(rim), pack(edge)], axis=0), "view", 3)
        from_c = swap(jnp.concatenate([pack(overlap(rim)), pack(overlap(edge))], axis=0), "view", 2)
        z_edge, z_rim = jnp.split(unpack(from_z, rad), 2, axis=0)
        c_edge, c_rim = jnp.split(unpack(from_c, rad), 2, axis=0)

        def spread(value):
            return lax.dynamic_update_slice_in_dim(jnp.zeros((wy,) + value.shape[1:], value.dtype), value, start, 0)

        def widen(value):
            empty = jnp.zeros(value.shape[:-1] + (hz - rad,), value.dtype)
            return jnp.where(
                zh == 0,
                jnp.concatenate([empty, value], axis=-1),
                jnp.concatenate([value, empty], axis=-1),
            )

        main = main + spread(from_y[:hy]) + widen(z_edge + spread(c_edge))
        rim = rim + spread(unpack(from_y[hy:], rad)) + z_rim + spread(c_rim)
        total = jnp.concatenate([main, pack(rim)], axis=0)
        estimate = estimate * total / count[None, :, None]

    own = lax.dynamic_slice_in_dim(estimate, rad * yh, hy, axis=0)
    parts = lax.all_gather(own, "view")
    low = jnp.concatenate([parts[0], parts[1]], axis=0)
    high = jnp.concatenate([parts[3], parts[2]], axis=0)
    return jnp.concatenate([low, high], axis=-1).transpose(1, 0, 2)


def solution(mesh):
    return jax.shard_map(
        body,
        mesh=mesh,
        in_specs=(
            P("space", None, None),
            P("view", "space", None, None),
            P("view", None, None),
            P("view"),
            P("view", "space"),
        ),
        out_specs=P("space", None, None),
        check_vma=False,
    )
```

```python
import functools

import jax
import jax.numpy as jnp
from jax import lax
from jax.experimental import pallas as pl
from jax.experimental.pallas import tpu as pltpu
from jax.sharding import PartitionSpec as P

ITERS = 2
LANES = 128
BLOCK = 8
F32, BF16 = jnp.float32, jnp.bfloat16
PARAMS = pltpu.CompilerParams(vmem_limit_bytes=58 * 1024 * 1024)


def swap(value, axis, mask):
    count = lax.axis_size(axis)
    return lax.ppermute(value, axis, [(i, i ^ mask) for i in range(count)])


def pick(kern, index):
    hit = index[..., None] == jnp.arange(kern.shape[-1])
    lead = kern.reshape(kern.shape[:1] + (1,) * (index.ndim - 1) + kern.shape[1:])
    return jnp.sum(jnp.where(hit, lead, 0.0), axis=-1)


def orders(bits):
    shift = (bits - 1) // 2
    upper = list(range(1, bits))
    return upper, upper[shift:] + upper[:shift]


def scatter_sum(kept, sent):
    bits = lax.axis_size("space").bit_length() - 1
    blocks = kept + swap(sent, "space", 1)
    middle = blocks.shape[1] // 2
    out = []
    for part, order in zip((blocks[:, :middle], blocks[:, middle:]), orders(bits)):
        left = list(range(1, bits))
        for bit in order:
            low = 1 << left.index(bit)
            split = part.reshape((part.shape[0] // (2 * low), 2, low) + part.shape[1:])
            part = split[:, 0] + swap(split[:, 1], "space", 1 << bit)
            part = part.reshape((-1,) + part.shape[2:])
            left.remove(bit)
        out.append(part[0])
    return out


def gather(parts):
    bits = lax.axis_size("space").bit_length() - 1
    out = []
    for part, order in zip(parts, orders(bits)):
        part = part[None]
        have = []
        for bit in reversed(order):
            low = 1 << sum(other < bit for other in have)
            part = part.reshape((part.shape[0] // low, 1, low) + part.shape[1:])
            part = jnp.concatenate([part, swap(part, "space", 1 << bit)], axis=1)
            part = part.reshape((-1,) + part.shape[3:])
            have.append(bit)
        out += [part, swap(part, "space", 1)]
    return out


def split(value):
    high = value.astype(BF16)
    return high, (value - high.astype(F32)).astype(BF16)


def stack3(value):
    high, low = split(value)
    return jnp.concatenate([high, low, high], axis=0)


def mul(a, b):
    return jnp.dot(a, b, preferred_element_type=F32)


def mul3(value, high, low):
    a, b = split(value)
    return mul(a, high) + mul(b, high) + mul(a, low)


def lane_of(shape):
    return lax.broadcasted_iota(jnp.int32, shape, len(shape) - 1)


def ahead_kernel(rad, place, ky, wx, kzh, kzl, a0, a1, b0, b1, blurred, u, uh, zp):
    yh = place[0]
    wy, nvi, hz = u.shape
    hy = blurred.shape[0]
    width = a0.shape[2]
    nviews = nvi // width
    half, group = wy // 2, hz // rad
    for h, pair in enumerate(((a0, a1), (b0, b1))):

        def row(y):
            return jnp.concatenate([ref[k, y] for ref in pair for k in range(ref.shape[0])], axis=0)

        rims = half // group
        for k in range(rims):
            out = mul(wx[...], stack3(row(half + k)))
            for m in range(group):
                uh[h * half + k * group + m] = out if m == 0 else pltpu.roll(out, hz - rad * m, 1)

        def two(p, carry):
            out = mul(wx[...], stack3(jnp.concatenate([row(2 * p), row(2 * p + 1)], axis=1)))
            u[h * half + 2 * p] = out[:, :hz]
            u[h * half + 2 * p + 1] = out[:, hz:]
            return carry

        lax.fori_loop(0, half // 2, two, 0)

    lead = rad * (1 - yh)
    zp[pl.ds((wy) * yh, rad)] = jnp.zeros((rad, nvi, hz), F32)

    def one(v, carry):
        at = pl.ds(pl.multiple_of(v * width, width), width)
        for c in range(2):
            rows = pl.ds(c * half, half)
            value = jnp.concatenate([u[rows, at, :], uh[rows, at, :]], axis=-1)
            out = mul3(value.reshape(half * width, 2 * hz), kzh[v], kzl[v])
            zp[pl.ds(lead + c * half, half), at, :] = out.reshape(half, width, hz)
        return carry

    lax.fori_loop(0, nviews, one, 0)

    def tile(s, carry):
        v = s // (width // 8)
        at = pl.ds(pl.multiple_of(s * 8, 8), 8)
        tap = [ky[v, t] for t in range(2 * rad)]
        for first in range(0, hy, BLOCK):
            total = [None] * BLOCK
            for y in range(first, first + BLOCK + 2 * rad - 1):
                value = zp[y, at, :]
                for k in range(BLOCK):
                    t = y - first - k
                    if 0 <= t < 2 * rad:
                        term = tap[t] * value
                        total[k] = term if total[k] is None else total[k] + term
            for k in range(BLOCK):
                blurred[first + k, at, :] = total[k]
        return carry

    lax.fori_loop(0, nvi // 8, tile, 0)


def back_kernel(rad, npieces, place, ky, wxt, kzh, kzl, blurred, *refs):
    pieces, (kept, sent, r, yb, gm, gh) = refs[:npieces], refs[npieces:]
    yh = place[0]
    hy, nvi, hz = blurred.shape
    wy = gm.shape[0]
    local, width = pieces[0].shape[:2]
    nviews = nvi // width
    half, group = wy // 2, hz // rad
    rims = half // group
    for p, piece in enumerate(pieces):
        for k in range(local):
            first = (p * local + k) * width
            for y in range(hy):
                r[y, first : first + width, :] = piece[k, :, y, :] / blurred[y, first : first + width, :]

    def tile(s, carry):
        v = s // (width // 8)
        at = pl.ds(pl.multiple_of(s * 8, 8), 8)
        tap = [ky[v, t] for t in range(2 * rad)]
        for first in range(0, hy + 2 * rad, BLOCK):
            total = [None] * BLOCK
            for y in range(max(0, first - 2 * rad + 1), min(hy, first + BLOCK)):
                value = r[y, at, :]
                for k in range(BLOCK):
                    t = first + k - y
                    if 0 <= t < 2 * rad:
                        term = tap[t] * value
                        total[k] = term if total[k] is None else total[k] + term
            for k in range(BLOCK):
                yb[first + k, at, :] = jnp.zeros((8, hz), F32) if total[k] is None else total[k]
        return carry

    lax.fori_loop(0, nvi // 8, tile, 0)

    lead = rad * (1 - yh)

    def one(v, carry):
        at = pl.ds(pl.multiple_of(v * width, width), width)
        for c in range(2):
            value = yb[pl.ds(lead + c * half, half), at, :].reshape(half * width, hz)
            out = mul3(value, kzh[v], kzl[v]).reshape(half, width, 2 * hz)
            gm[pl.ds(c * half, half), at, :] = out[..., :hz]
            for k in range(rims):
                total = out[k * group, :, hz:]
                for m in range(1, group):
                    total = total + pltpu.roll(out[k * group + m, :, hz:], rad * m, 1)
                gh[c * rims + k, at, :] = total
        return carry

    lax.fori_loop(0, nviews, one, 0)

    def store(out, row):
        for c, ref in enumerate((kept, sent)):
            for k in range(ref.shape[0]):
                first = (c * ref.shape[0] + k) * width
                ref[k, row] = out[first : first + width]

    for c in range(2):
        for k in range(rims):
            store(mul(wxt[...], stack3(gh[c * rims + k])), c * (half + rims) + half + k)

        def two(p, carry):
            y = c * half + 2 * p
            out = mul(wxt[...], stack3(jnp.concatenate([gm[y], gm[y + 1]], axis=1)))
            row = c * (half + rims) + 2 * p
            store(out[:, :hz], row)
            store(out[:, hz:], row + 1)
            return carry

        lax.fori_loop(0, half // 2, two, 0)


def row_of(a, b, y, half):
    return a[y] if y < half else b[y - half]


def pack_kernel(rad, place, a, b, to_y, to_z, to_c, edge):
    yh, zh = place[0], place[1]
    rows, width, hz = a.shape
    group = hz // rad
    half = rows * group // (group + 1)
    rims, wy = half // group, 2 * half
    begin = (hz - rad) * (1 - zh)
    lane = lane_of((width, hz)) // rad
    for o in range(2 * rims):
        total = None
        for m in range(group):
            value = pltpu.roll(row_of(a, b, o * group + m, half), (rad * m - begin + hz) % hz, 1)
            total = value if m == 0 else jnp.where(lane == m, value, total)
        edge[o] = total
        to_z[2 * rims + o] = total
        to_z[o] = (a if o < rims else b)[half + o % rims]
    hy = wy - rad
    over = hy // group
    for y in range(wy):
        @pl.when(jnp.logical_and(y >= rad * (1 - yh), y < rad * (1 - yh) + hy))
        def _():
            to_y[y - rad * (1 - yh)] = row_of(a, b, y, half)
    skip = (rad // group) * (1 - yh)
    for k in range(over):
        to_y[hy + k] = to_z[skip + k]
        to_c[k] = to_z[skip + k]
        to_c[over + k] = edge[skip + k]


def update_kernel(rad, place, a, b, fy, fz, fc, old, count, new):
    yh, zh = place[0], place[1]
    rows, width, hz = a.shape
    group = hz // rad
    half = rows * group // (group + 1)
    rims, wy = half // group, 2 * half
    hy = wy - rad
    over = hy // group
    start, skip = rad * (1 - yh), (rad // group) * (1 - yh)
    begin = (hz - rad) * (1 - zh)
    zero = jnp.zeros((width, hz), F32)
    inside = (lane_of((width, hz)) >= begin) & (lane_of((width, hz)) < begin + rad)
    total = count[...]

    def part(ref, first, at, limit):
        ok = jnp.logical_and(at >= 0, at < limit)
        return jnp.where(ok, ref[first + jnp.clip(at, 0, limit - 1)], zero)

    for o in range(2 * rims):
        h, k = o // rims, o % rims
        row = h * rows + half + k
        rim = (a, b)[h][half + k] + fz[2 * rims + o]
        rim = rim + part(fy, hy, o - skip, over) + part(fc, over, o - skip, over)
        new[row] = old[row] * rim / total
        edge = fz[o] + part(fc, 0, o - skip, over)
        for m in range(group):
            y = o * group + m
            moved = jnp.where(inside, pltpu.roll(edge, (begin - rad * m + hz) % hz, 1), 0.0)
            value = row_of(a, b, y, half) + part(fy, 0, y - start, hy) + moved
            row = h * rows + y - h * half
            new[row] = old[row] * value / total


VMEM = pl.BlockSpec(memory_space=pltpu.VMEM)
SMEM = pl.BlockSpec(memory_space=pltpu.SMEM)


def call(kernel, shapes, scratch, smem, cost, *args):
    flops, moved = cost
    return pl.pallas_call(
        kernel,
        out_shape=[jax.ShapeDtypeStruct(shape, F32) for shape in shapes],
        in_specs=[SMEM] * smem + [VMEM] * (len(args) - smem),
        out_specs=[VMEM] * len(shapes),
        scratch_shapes=[pltpu.VMEM(shape, F32) for shape in scratch],
        compiler_params=PARAMS,
        cost_estimate=pl.CostEstimate(flops=flops, bytes_accessed=moved, transcendentals=0),
    )(*args)


def body(prior, data, taps, offsets, coverage):
    nview, nspace = lax.axis_size("view"), lax.axis_size("space")
    g, j = lax.axis_index("view"), lax.axis_index("space")
    zh, yh = g >> 1, (g ^ (g >> 1)) & 1
    place_yz = jnp.stack([yh, zh]).astype(jnp.int32)
    local, width, ny, nz = data.shape
    ntaps = taps.shape[-1]
    rad = ntaps // 2
    hy, hz = ny // 2, nz // 2
    wy = hy + rad
    group = hz // rad
    half, rims = wy // 2, wy // 2 // group
    rows = half + rims

    flat = jnp.concatenate(
        [
            taps.reshape(local, -1),
            offsets.astype(jnp.float32)[:, None],
            coverage.astype(jnp.float32),
        ],
        axis=1,
    )
    used = flat.shape[1]
    flat = jnp.pad(flat, ((0, 0), (0, -used % LANES)))
    shared = [flat] + [swap(flat, "view", r) for r in range(1, nview)]
    *shared, data = lax.optimization_barrier((*shared, data))
    shared = jnp.concatenate(shared, axis=0)

    def quadrant(owner):
        oz, oy = owner >> 1, (owner ^ (owner >> 1)) & 1
        return lax.dynamic_slice(data, (0, 0, oy * hy, oz * hz), (local, width, hy, hz))

    pieces = [quadrant(g)] + [swap(quadrant(g ^ r), "view", r) for r in range(1, nview)]

    nviews = nview * local
    nvi = nviews * width
    kern = shared[:, : 3 * ntaps].reshape(nviews, 3, ntaps)
    kern = kern / jnp.sum(kern, axis=-1, keepdims=True)
    turn = shared[:, 3 * ntaps].astype(jnp.int32)
    cover = shared[:, 3 * ntaps + 1 : used]
    count = jnp.broadcast_to(jnp.sum(cover, axis=0)[:, None], (width, hz))
    note = jnp.pad(cover.T, ((0, 0), (0, hz - nviews)))[None]

    window = lax.dynamic_slice_in_dim(prior, rad * yh, wy, axis=1).transpose(1, 0, 2)
    main = lax.dynamic_slice_in_dim(window, hz * zh, hz, axis=2)
    rim = lax.dynamic_slice_in_dim(window, jnp.where(zh == 0, hz, hz - rad), rad, axis=2)
    rim = rim.reshape(2 * rims, group, width, rad).transpose(0, 2, 1, 3).reshape(2 * rims, width, hz)
    parts = [main[:half], rim[:rims], main[half:], rim[rims:]]
    estimate = jnp.concatenate(parts, axis=0)
    wide = gather([jnp.concatenate(parts[:2] + [note], axis=0), jnp.concatenate(parts[2:], axis=0)])
    cover = jnp.stack([wide[0][:, -1], wide[1][:, -1]])[..., :nviews]
    cover = cover.transpose(3, 0, 1, 2).reshape(nviews, 1, nspace * width)

    slab = (j - turn) % nspace
    spot = slab[:, None] * width + jnp.arange(width)
    order = jnp.arange(nspace).reshape(nspace // 2, 2).T.reshape(-1)
    planes = ((j ^ order)[:, None] * width + jnp.arange(width)).reshape(-1)
    band_x = pick(kern[:, 0], planes - spot[:, :, None] + rad)
    band_xt = (band_x * cover).reshape(nvi, -1).T
    band_x = band_x.reshape(nvi, -1)

    def halves(value):
        high = lax.reduce_precision(value, 8, 7)
        return high.astype(BF16), (value - high).astype(BF16)

    def triple(value):
        high, low = halves(value)
        return jnp.concatenate([high, high, low], axis=1)

    wx, wxt = triple(band_x), triple(band_xt)
    cells = jnp.concatenate([jnp.arange(hz) + hz * zh, jnp.arange(hz) + jnp.where(zh == 0, hz, hz - rad)])
    real = jnp.arange(2 * hz) < hz + rad
    goal = jnp.arange(hz) + hz * zh
    index = jnp.where(real[:, None], cells[:, None] - goal + rad, -1)
    band_z = pick(kern[:, 2], index[None])
    kz = halves(band_z)
    kzt = halves(band_z.transpose(0, 2, 1))
    ky = kern[:, 1]

    plane = width * hz
    mxu = 2 * 3 * nvi * plane * 2 * rows * (nspace // 2)

    def ahead(wide):
        return call(
            functools.partial(ahead_kernel, rad),
            [(hy, nvi, hz)],
            [(wy, nvi, hz), (wy, nvi, hz), (wy + rad, nvi, hz)],
            2,
            (mxu, 4 * plane * (nspace * 2 * rows + hy * nviews)),
            place_yz, ky, wx, *kz, *wide,
        )[0]

    def back(blurred):
        return call(
            functools.partial(back_kernel, rad, nview),
            [(nspace // 2, 2 * rows, width, hz)] * 2,
            [(hy, nvi, hz), (hy + 2 * rad, nvi, hz), (wy, nvi, hz), (2 * rims, nvi, hz)],
            2,
            (mxu, 4 * plane * (nspace * 2 * rows + 2 * hy * nviews)),
            place_yz, ky, wxt, *kzt, blurred, *pieces,
        )

    over = hy // group
    for step in range(ITERS):
        if step:
            wide = gather([estimate[:rows], estimate[rows:]])
        a, b = scatter_sum(*back(ahead(wide)))
        to_y, to_z, to_c = call(
            functools.partial(pack_kernel, rad),
            [(hy + over, width, hz), (4 * rims, width, hz), (2 * over, width, hz)],
            [(2 * rims, width, hz)],
            1,
            (plane, 4 * plane * 4 * rows),
            place_yz, a, b,
        )
        estimate = call(
            functools.partial(update_kernel, rad),
            [(2 * rows, width, hz)],
            [],
            1,
            (plane, 4 * plane * 8 * rows),
            place_yz, a, b, swap(to_y, "view", 1), swap(to_z, "view", 3), swap(to_c, "view", 2), estimate, count,
        )[0]

    main = jnp.concatenate([estimate[:half], estimate[rows : rows + half]], axis=0)
    own = lax.dynamic_slice_in_dim(main, rad * yh, hy, axis=0)
    parts = lax.all_gather(own, "view")
    low = jnp.concatenate([parts[0], parts[1]], axis=0)
    high = jnp.concatenate([parts[3], parts[2]], axis=0)
    return jnp.concatenate([low, high], axis=-1).transpose(1, 0, 2)


def solution(mesh):
    return jax.shard_map(
        body,
        mesh=mesh,
        in_specs=(
            P("space", None, None),
            P("view", "space", None, None),
            P("view", None, None),
            P("view"),
            P("view", "space"),
        ),
        out_specs=P("space", None, None),
        check_vma=False,
    )
```

```python
import functools

import jax
import jax.numpy as jnp
from jax import lax
from jax.experimental import pallas as pl
from jax.experimental.pallas import tpu as pltpu
from jax.sharding import PartitionSpec as P

ITERS = 2
LANES = 128
BLOCK = 8
F32, BF16 = jnp.float32, jnp.bfloat16
PARAMS = pltpu.CompilerParams(vmem_limit_bytes=58 * 1024 * 1024)


def swap(value, axis, mask):
    count = lax.axis_size(axis)
    return lax.ppermute(value, axis, [(i, i ^ mask) for i in range(count)])


def pick(kern, index):
    hit = index[..., None] == jnp.arange(kern.shape[-1])
    lead = kern.reshape(kern.shape[:1] + (1,) * (index.ndim - 1) + kern.shape[1:])
    return jnp.sum(jnp.where(hit, lead, 0.0), axis=-1)


def orders(bits):
    shift = (bits - 1) // 2
    upper = list(range(1, bits))
    return upper, upper[shift:] + upper[:shift]


def scatter_sum(kept, sent):
    bits = lax.axis_size("space").bit_length() - 1
    blocks = kept + swap(sent, "space", 1)
    middle = blocks.shape[1] // 2
    out = []
    for part, order in zip((blocks[:, :middle], blocks[:, middle:]), orders(bits)):
        left = list(range(1, bits))
        for bit in order:
            low = 1 << left.index(bit)
            split = part.reshape((part.shape[0] // (2 * low), 2, low) + part.shape[1:])
            part = split[:, 0] + swap(split[:, 1], "space", 1 << bit)
            part = part.reshape((-1,) + part.shape[2:])
            left.remove(bit)
        out.append(part[0])
    return out


def gather(parts):
    bits = lax.axis_size("space").bit_length() - 1
    out = []
    for part, order in zip(parts, orders(bits)):
        part = part[None]
        have = []
        for bit in reversed(order):
            low = 1 << sum(other < bit for other in have)
            part = part.reshape((part.shape[0] // low, 1, low) + part.shape[1:])
            part = jnp.concatenate([part, swap(part, "space", 1 << bit)], axis=1)
            part = part.reshape((-1,) + part.shape[3:])
            have.append(bit)
        out += [part, swap(part, "space", 1)]
    return out


def split(value):
    high = value.astype(BF16)
    return high, (value - high.astype(F32)).astype(BF16)


def stack3(value):
    high, low = split(value)
    return jnp.concatenate([high, low, high], axis=0)


def mul(a, b):
    return jnp.dot(a, b, preferred_element_type=F32)


def lane_of(shape):
    return lax.broadcasted_iota(jnp.int32, shape, len(shape) - 1)


def ahead_kernel(rad, place, ky, wx, kz, a0, a1, b0, b1, *refs):
    blurred, u, uh, za, zb = refs[-5:]
    yh = place[0]
    wy, nvi, hz = u.shape
    hy = blurred.shape[0]
    width = a0.shape[2]
    nviews = nvi // width
    half, group = wy // 2, hz // rad
    part = lane_of((nvi, hz)) // rad
    for h, pair in enumerate(((a0, a1), (b0, b1))):

        def row(y):
            return jnp.concatenate([ref[k, y] for ref in pair for k in range(ref.shape[0])], axis=0)

        for k in range(half // group):
            out = mul(wx[...], stack3(row(half + k)))
            high = out.astype(BF16).astype(F32)
            low = out - high
            for m in range(group):
                first, second, third = (
                    pltpu.roll(value, (rad * (at - m)) % hz, 1) if at != m else value
                    for at, value in enumerate((high, low, high))
                )
                value = jnp.where(part == 0, first, jnp.where(part == 1, second, jnp.where(part == 2, third, 0.0)))
                uh[h * half + k * group + m] = value.astype(BF16)

        def two(p, carry):
            out = mul(wx[...], stack3(jnp.concatenate([row(2 * p), row(2 * p + 1)], axis=1)))
            u[h * half + 2 * p] = out[:, :hz]
            u[h * half + 2 * p + 1] = out[:, hz:]
            return carry

        lax.fori_loop(0, half // 2, two, 0)

    lead = rad * (1 - yh)
    for z in (za, zb):
        z[pl.ds(wy * yh, rad)] = jnp.zeros((rad, width, hz), F32)

    def along_z(v, z):
        at = pl.ds(pl.multiple_of(v * width, width), width)
        high, low = split(u[:, at, :].reshape(wy * width, hz))
        value = jnp.concatenate([high, low, high, uh[:, at, :].reshape(wy * width, hz)], axis=1)
        z[pl.ds(lead, wy)] = mul(value, kz[v]).reshape(wy, width, hz)

    def along_y(v, z):
        tap = [ky[v, t] for t in range(2 * rad)]
        for s in range(0, width, 8):
            for first in range(0, hy, BLOCK):
                total = [None] * BLOCK
                for y in range(first, first + BLOCK + 2 * rad - 1):
                    value = z[y, s : s + 8, :]
                    for k in range(BLOCK):
                        t = y - first - k
                        if 0 <= t < 2 * rad:
                            term = tap[t] * value
                            total[k] = term if total[k] is None else total[k] + term
                for k in range(BLOCK):
                    blurred[first + k, pl.ds(pl.multiple_of(v * width + s, 8), 8), :] = total[k]

    along_z(0, za)

    def views(p, carry):
        along_z(2 * p + 1, zb)
        along_y(2 * p, za)
        along_z(jnp.minimum(2 * p + 2, nviews - 1), za)
        along_y(2 * p + 1, zb)
        return carry

    lax.fori_loop(0, nviews // 2, views, 0)


def back_kernel(rad, npieces, place, ky, wxt, kz, blurred, *refs):
    pieces, (kept, sent, r, ya, yb, gm, gh) = refs[:npieces], refs[npieces:]
    yh = place[0]
    hy, nvi, hz = blurred.shape
    wy = gm.shape[0]
    local, width = pieces[0].shape[:2]
    nviews = nvi // width
    half, group = wy // 2, hz // rad
    rims = half // group
    for p, piece in enumerate(pieces):
        for k in range(local):
            first = (p * local + k) * width
            for y in range(hy):
                r[y, first : first + width, :] = piece[k, :, y, :] / blurred[y, first : first + width, :]

    lead = rad * (1 - yh)

    def along_y(v, out):
        tap = [ky[v, t] for t in range(2 * rad)]
        for s in range(0, width, 8):
            at = pl.ds(pl.multiple_of(v * width + s, 8), 8)
            for first in range(0, hy + 2 * rad, BLOCK):
                total = [None] * BLOCK
                for y in range(max(0, first - 2 * rad + 1), min(hy, first + BLOCK)):
                    value = r[y, at, :]
                    for k in range(BLOCK):
                        t = first + k - y
                        if 0 <= t < 2 * rad:
                            term = tap[t] * value
                            total[k] = term if total[k] is None else total[k] + term
                for k in range(BLOCK):
                    out[first + k, s : s + 8, :] = jnp.zeros((8, hz), F32) if total[k] is None else total[k]

    def along_z(v, y):
        at = pl.ds(pl.multiple_of(v * width, width), width)
        high, low = split(y[pl.ds(lead, wy)].reshape(wy * width, hz))
        out = mul(jnp.concatenate([high, low, high], axis=1), kz[v]).reshape(wy, width, 2 * hz)
        gm[:, at, :] = out[..., :hz]
        for o in range(2 * rims):
            total = out[o * group, :, hz:]
            for m in range(1, group):
                total = total + pltpu.roll(out[o * group + m, :, hz:], rad * m, 1)
            gh[o, at, :] = total

    along_y(0, ya)

    def views(p, carry):
        along_y(2 * p + 1, yb)
        along_z(2 * p, ya)
        along_y(jnp.minimum(2 * p + 2, nviews - 1), ya)
        along_z(2 * p + 1, yb)
        return carry

    lax.fori_loop(0, nviews // 2, views, 0)

    def store(out, row):
        for c, ref in enumerate((kept, sent)):
            for k in range(ref.shape[0]):
                first = (c * ref.shape[0] + k) * width
                ref[k, row] = out[first : first + width]

    for c in range(2):
        for k in range(rims):
            store(mul(wxt[...], stack3(gh[c * rims + k])), c * (half + rims) + half + k)

        def two(p, carry):
            y = c * half + 2 * p
            out = mul(wxt[...], stack3(jnp.concatenate([gm[y], gm[y + 1]], axis=1)))
            row = c * (half + rims) + 2 * p
            store(out[:, :hz], row)
            store(out[:, hz:], row + 1)
            return carry

        lax.fori_loop(0, half // 2, two, 0)


def row_of(a, b, y, half):
    return a[y] if y < half else b[y - half]


def pack_kernel(rad, place, a, b, to_y, to_z, to_c, edge):
    yh, zh = place[0], place[1]
    rows, width, hz = a.shape
    group = hz // rad
    half = rows * group // (group + 1)
    rims, wy = half // group, 2 * half
    begin = (hz - rad) * (1 - zh)
    lane = lane_of((width, hz)) // rad
    for o in range(2 * rims):
        total = None
        for m in range(group):
            value = pltpu.roll(row_of(a, b, o * group + m, half), (rad * m - begin + hz) % hz, 1)
            total = value if m == 0 else jnp.where(lane == m, value, total)
        edge[o] = total
        to_z[2 * rims + o] = total
        to_z[o] = (a if o < rims else b)[half + o % rims]
    hy = wy - rad
    over = hy // group
    for y in range(wy):
        @pl.when(jnp.logical_and(y >= rad * (1 - yh), y < rad * (1 - yh) + hy))
        def _():
            to_y[y - rad * (1 - yh)] = row_of(a, b, y, half)
    skip = (rad // group) * (1 - yh)
    for k in range(over):
        to_y[hy + k] = to_z[skip + k]
        to_c[k] = to_z[skip + k]
        to_c[over + k] = edge[skip + k]


def update_kernel(rad, place, a, b, fy, fz, fc, old, count, new):
    yh, zh = place[0], place[1]
    rows, width, hz = a.shape
    group = hz // rad
    half = rows * group // (group + 1)
    rims, wy = half // group, 2 * half
    hy = wy - rad
    over = hy // group
    start, skip = rad * (1 - yh), (rad // group) * (1 - yh)
    begin = (hz - rad) * (1 - zh)
    zero = jnp.zeros((width, hz), F32)
    inside = (lane_of((width, hz)) >= begin) & (lane_of((width, hz)) < begin + rad)
    total = count[...]

    def part(ref, first, at, limit):
        ok = jnp.logical_and(at >= 0, at < limit)
        return jnp.where(ok, ref[first + jnp.clip(at, 0, limit - 1)], zero)

    for o in range(2 * rims):
        h, k = o // rims, o % rims
        row = h * rows + half + k
        rim = (a, b)[h][half + k] + fz[2 * rims + o]
        rim = rim + part(fy, hy, o - skip, over) + part(fc, over, o - skip, over)
        new[row] = old[row] * rim / total
        edge = fz[o] + part(fc, 0, o - skip, over)
        for m in range(group):
            y = o * group + m
            moved = jnp.where(inside, pltpu.roll(edge, (begin - rad * m + hz) % hz, 1), 0.0)
            value = row_of(a, b, y, half) + part(fy, 0, y - start, hy) + moved
            row = h * rows + y - h * half
            new[row] = old[row] * value / total


def assemble_kernel(where, *refs):
    pieces, out = refs[:-1], refs[-1]
    hy, width, hz = pieces[0].shape
    for r, piece in enumerate(pieces):
        for owner in range(len(pieces)):
            oz, oy = owner >> 1, (owner ^ (owner >> 1)) & 1

            @pl.when(where[0] == owner ^ r)
            def _():
                for y in range(hy):
                    out[:, oy * hy + y, oz * hz : (oz + 1) * hz] = piece[y]


VMEM = pl.BlockSpec(memory_space=pltpu.VMEM)
ANY = pl.BlockSpec(memory_space=pl.ANY)
SMEM = pl.BlockSpec(memory_space=pltpu.SMEM)


def call(kernel, shapes, scratch, smem, cost, *args, late=()):
    flops, moved = cost
    return pl.pallas_call(
        kernel,
        out_shape=[jax.ShapeDtypeStruct(shape, F32) for shape in shapes],
        in_specs=[SMEM] * smem + [VMEM] * (len(args) - smem) + [ANY] * len(late),
        out_specs=[VMEM] * len(shapes),
        scratch_shapes=[pltpu.VMEM(s, F32) if isinstance(s, tuple) else s for s in scratch],
        compiler_params=PARAMS,
        cost_estimate=pl.CostEstimate(flops=flops, bytes_accessed=moved, transcendentals=0),
    )(*args, *late)


def body(prior, data, taps, offsets, coverage):
    nview, nspace = lax.axis_size("view"), lax.axis_size("space")
    g, j = lax.axis_index("view"), lax.axis_index("space")
    zh, yh = g >> 1, (g ^ (g >> 1)) & 1
    place_yz = jnp.stack([yh, zh]).astype(jnp.int32)
    local, width, ny, nz = data.shape
    ntaps = taps.shape[-1]
    rad = ntaps // 2
    hy, hz = ny // 2, nz // 2
    wy = hy + rad
    group = hz // rad
    half, rims = wy // 2, wy // 2 // group
    rows = half + rims

    flat = jnp.concatenate(
        [
            taps.reshape(local, -1),
            offsets.astype(jnp.float32)[:, None],
            coverage.astype(jnp.float32),
        ],
        axis=1,
    )
    used = flat.shape[1]
    flat = jnp.pad(flat, ((0, 0), (0, -used % LANES)))
    shared = [flat] + [swap(flat, "view", r) for r in range(1, nview)]
    shared = jnp.concatenate(shared, axis=0)

    def quadrant(owner):
        oz, oy = owner >> 1, (owner ^ (owner >> 1)) & 1
        return lax.dynamic_slice(data, (0, 0, oy * hy, oz * hz), (local, width, hy, hz))

    pieces = [quadrant(g)] + [swap(quadrant(g ^ r), "view", r) for r in range(1, nview)]

    nviews = nview * local
    nvi = nviews * width
    kern = shared[:, : 3 * ntaps].reshape(nviews, 3, ntaps)
    kern = kern / jnp.sum(kern, axis=-1, keepdims=True)
    turn = shared[:, 3 * ntaps].astype(jnp.int32)
    cover = shared[:, 3 * ntaps + 1 : used]
    count = jnp.broadcast_to(jnp.sum(cover, axis=0)[:, None], (width, hz))
    note = jnp.pad(cover.T, ((0, 0), (0, hz - nviews)))[None]

    window = lax.dynamic_slice_in_dim(prior, rad * yh, wy, axis=1).transpose(1, 0, 2)
    main = lax.dynamic_slice_in_dim(window, hz * zh, hz, axis=2)
    rim = lax.dynamic_slice_in_dim(window, jnp.where(zh == 0, hz, hz - rad), rad, axis=2)
    rim = rim.reshape(2 * rims, group, width, rad).transpose(0, 2, 1, 3).reshape(2 * rims, width, hz)
    parts = [main[:half], rim[:rims], main[half:], rim[rims:]]
    estimate = jnp.concatenate(parts, axis=0)
    wide = gather([jnp.concatenate(parts[:2] + [note], axis=0), jnp.concatenate(parts[2:], axis=0)])
    cover = jnp.stack([wide[0][:, -1], wide[1][:, -1]])[..., :nviews]
    cover = cover.transpose(3, 0, 1, 2).reshape(nviews, 1, nspace * width)

    slab = (j - turn) % nspace
    spot = slab[:, None] * width + jnp.arange(width)
    order = jnp.arange(nspace).reshape(nspace // 2, 2).T.reshape(-1)
    planes = ((j ^ order)[:, None] * width + jnp.arange(width)).reshape(-1)
    band_x = pick(kern[:, 0], planes - spot[:, :, None] + rad)
    band_xt = (band_x * cover).reshape(nvi, -1).T
    band_x = band_x.reshape(nvi, -1)

    def halves(value):
        high = lax.reduce_precision(value, 8, 7)
        return high.astype(BF16), (value - high).astype(BF16)

    def triple(value):
        high, low = halves(value)
        return jnp.concatenate([high, high, low], axis=1)

    wx, wxt = triple(band_x), triple(band_xt)
    cells = jnp.concatenate([jnp.arange(hz) + hz * zh, jnp.arange(hz) + jnp.where(zh == 0, hz, hz - rad)])
    real = jnp.arange(2 * hz) < hz + rad
    goal = jnp.arange(hz) + hz * zh
    index = jnp.where(real[:, None], cells[:, None] - goal + rad, -1)
    band_z = pick(kern[:, 2], index[None])
    high, low = halves(band_z)
    kz = [high[:, :hz], high[:, :hz], low[:, :hz]]
    kz += [high[:, hz : hz + rad], high[:, hz : hz + rad], low[:, hz : hz + rad]]
    kz = jnp.concatenate(kz + [jnp.zeros((nviews, hz - 3 * rad, hz), BF16)], axis=1)
    high, low = halves(band_z.transpose(0, 2, 1))
    kzt = jnp.concatenate([high, high, low], axis=1)
    ky = kern[:, 1]

    plane = width * hz
    mxu = 2 * 3 * nvi * plane * 2 * rows * (nspace // 2)

    def ahead(wide, late, cost):
        return call(
            functools.partial(ahead_kernel, rad),
            [(hy, nvi, hz)],
            [(wy, nvi, hz), pltpu.VMEM((wy, nvi, hz), BF16), (wy + rad, width, hz), (wy + rad, width, hz)],
            2,
            cost,
            place_yz, ky, wx, kz, *wide,
            late=late,
        )[0]

    def back(blurred):
        return call(
            functools.partial(back_kernel, rad, nview),
            [(nspace // 2, 2 * rows, width, hz)] * 2,
            [(hy, nvi, hz), (hy + 2 * rad, width, hz), (hy + 2 * rad, width, hz), (wy, nvi, hz), (2 * rims, nvi, hz)],
            2,
            (mxu, 4 * plane * (nspace * 2 * rows + 2 * hy * nviews)),
            place_yz, ky, wxt, kzt, blurred, *pieces,
        )

    over = hy // group
    for step in range(ITERS):
        if step:
            wide = gather([estimate[:rows], estimate[rows:]])
        blurred = ahead(wide, () if step else tuple(pieces[1:3]), (mxu if step else 0, plane))
        a, b = scatter_sum(*back(blurred))
        to_y, to_z, to_c = call(
            functools.partial(pack_kernel, rad),
            [(hy + over, width, hz), (4 * rims, width, hz), (2 * over, width, hz)],
            [(2 * rims, width, hz)],
            1,
            (plane, 4 * plane * 4 * rows),
            place_yz, a, b,
        )
        estimate = call(
            functools.partial(update_kernel, rad),
            [(2 * rows, width, hz)],
            [],
            1,
            (plane, 4 * plane * 8 * rows),
            place_yz, a, b, swap(to_y, "view", 1), swap(to_z, "view", 3), swap(to_c, "view", 2), estimate, count,
        )[0]

    main = jnp.concatenate([estimate[:half], estimate[rows : rows + half]], axis=0)
    own = lax.dynamic_slice_in_dim(main, rad * yh, hy, axis=0)
    parts = [own] + [swap(own, "view", r) for r in range(1, nview)]
    return call(
        assemble_kernel,
        [(width, ny, nz)],
        [],
        1,
        (plane, 16 * plane * ny),
        g.astype(jnp.int32)[None], *parts,
    )[0]


def solution(mesh):
    return jax.shard_map(
        body,
        mesh=mesh,
        in_specs=(
            P("space", None, None),
            P("view", "space", None, None),
            P("view", None, None),
            P("view"),
            P("view", "space"),
        ),
        out_specs=P("space", None, None),
        check_vma=False,
    )
```

```python
import functools

import jax
import jax.numpy as jnp
from jax import lax
from jax.experimental import pallas as pl
from jax.experimental.pallas import tpu as pltpu
from jax.sharding import PartitionSpec as P

ITERS = 2
LANES = 128
BLOCK = 8
F32, BF16 = jnp.float32, jnp.bfloat16
PARAMS = pltpu.CompilerParams(vmem_limit_bytes=58 * 1024 * 1024)


def swap(value, axis, mask):
    count = lax.axis_size(axis)
    return lax.ppermute(value, axis, [(i, i ^ mask) for i in range(count)])


def pick(kern, index):
    hit = index[..., None] == jnp.arange(kern.shape[-1])
    lead = kern.reshape(kern.shape[:1] + (1,) * (index.ndim - 1) + kern.shape[1:])
    return jnp.sum(jnp.where(hit, lead, 0.0), axis=-1)


def orders(bits):
    shift = (bits - 1) // 2
    upper = list(range(1, bits))
    return upper, upper[shift:] + upper[:shift]


def scatter_sum(kept, sent):
    bits = lax.axis_size("space").bit_length() - 1
    blocks = kept + swap(sent, "space", 1)
    middle = blocks.shape[1] // 2
    out = []
    for part, order in zip((blocks[:, :middle], blocks[:, middle:]), orders(bits)):
        left = list(range(1, bits))
        for bit in order:
            low = 1 << left.index(bit)
            split = part.reshape((part.shape[0] // (2 * low), 2, low) + part.shape[1:])
            part = split[:, 0] + swap(split[:, 1], "space", 1 << bit)
            part = part.reshape((-1,) + part.shape[2:])
            left.remove(bit)
        out.append(part[0])
    return out


def gather(parts):
    bits = lax.axis_size("space").bit_length() - 1
    out = []
    for part, order in zip(parts, orders(bits)):
        part = part[None]
        have = []
        for bit in reversed(order):
            low = 1 << sum(other < bit for other in have)
            part = part.reshape((part.shape[0] // low, 1, low) + part.shape[1:])
            part = jnp.concatenate([part, swap(part, "space", 1 << bit)], axis=1)
            part = part.reshape((-1,) + part.shape[3:])
            have.append(bit)
        out += [part, swap(part, "space", 1)]
    return out


def split(value):
    high = value.astype(BF16)
    return high, (value - high.astype(F32)).astype(BF16)


def stack3(value):
    high, low = split(value)
    return jnp.concatenate([high, low, high], axis=0)


def mul(a, b):
    return jnp.dot(a, b, preferred_element_type=F32)


def lane_of(shape):
    return lax.broadcasted_iota(jnp.int32, shape, len(shape) - 1)


def ahead_kernel(rad, place, ky, wx, kz, a0, a1, b0, b1, *refs):
    blurred, u, uh, za, zb = refs[-5:]
    yh = place[0]
    wy, nvi, hz = u.shape
    hy = blurred.shape[0]
    width = a0.shape[2]
    nviews = nvi // width
    half, group = wy // 2, hz // rad
    part = lane_of((nvi, hz)) // rad
    for h, pair in enumerate(((a0, a1), (b0, b1))):

        def row(y):
            return jnp.concatenate([ref[k, y] for ref in pair for k in range(ref.shape[0])], axis=0)

        for k in range(half // group):
            out = mul(wx[...], stack3(row(half + k)))
            high = out.astype(BF16).astype(F32)
            low = out - high
            for m in range(group):
                first, second, third = (
                    pltpu.roll(value, (rad * (at - m)) % hz, 1) if at != m else value
                    for at, value in enumerate((high, low, high))
                )
                value = jnp.where(part == 0, first, jnp.where(part == 1, second, jnp.where(part == 2, third, 0.0)))
                uh[h * half + k * group + m] = value.astype(BF16)

        for y in range(0, half, 2):
            out = mul(wx[...], stack3(jnp.concatenate([row(y), row(y + 1)], axis=1)))
            u[h * half + y] = out[:, :hz]
            u[h * half + y + 1] = out[:, hz:]

    lead = rad * (1 - yh)
    for z in (za, zb):
        z[pl.ds(wy * yh, rad)] = jnp.zeros((rad, width, hz), F32)

    def along_z(v, z):
        at = pl.ds(pl.multiple_of(v * width, width), width)
        high, low = split(u[:, at, :].reshape(wy * width, hz))
        value = jnp.concatenate([high, low, high, uh[:, at, :].reshape(wy * width, hz)], axis=1)
        z[pl.ds(lead, wy)] = mul(value, kz[v]).reshape(wy, width, hz)

    def along_y(v, z):
        tap = [ky[v, t] for t in range(2 * rad)]
        for s in range(0, width, 8):
            for first in range(0, hy, BLOCK):
                total = [None] * BLOCK
                for y in range(first, first + BLOCK + 2 * rad - 1):
                    value = z[y, s : s + 8, :]
                    for k in range(BLOCK):
                        t = y - first - k
                        if 0 <= t < 2 * rad:
                            term = tap[t] * value
                            total[k] = term if total[k] is None else total[k] + term
                for k in range(BLOCK):
                    blurred[first + k, pl.ds(pl.multiple_of(v * width + s, 8), 8), :] = total[k]

    along_z(0, za)

    def views(p, carry):
        along_z(2 * p + 1, zb)
        along_y(2 * p, za)
        along_z(jnp.minimum(2 * p + 2, nviews - 1), za)
        along_y(2 * p + 1, zb)
        return carry

    lax.fori_loop(0, nviews // 2, views, 0)


def back_kernel(rad, npieces, place, ky, wxt, kz, blurred, *refs):
    pieces, (kept, sent, r, ya, yb, gm, gh) = refs[:npieces], refs[npieces:]
    yh = place[0]
    hy, nvi, hz = blurred.shape
    wy = gm.shape[0]
    local, width = pieces[0].shape[:2]
    nviews = nvi // width
    half, group = wy // 2, hz // rad
    rims = half // group
    for p, piece in enumerate(pieces):
        for k in range(local):
            first = (p * local + k) * width
            for y in range(hy):
                r[y, first : first + width, :] = piece[k, :, y, :] / blurred[y, first : first + width, :]

    lead = rad * (1 - yh)

    def along_y(v, out):
        tap = [ky[v, t] for t in range(2 * rad)]
        for s in range(0, width, 8):
            at = pl.ds(pl.multiple_of(v * width + s, 8), 8)
            for first in range(0, hy + 2 * rad, BLOCK):
                total = [None] * BLOCK
                for y in range(max(0, first - 2 * rad + 1), min(hy, first + BLOCK)):
                    value = r[y, at, :]
                    for k in range(BLOCK):
                        t = first + k - y
                        if 0 <= t < 2 * rad:
                            term = tap[t] * value
                            total[k] = term if total[k] is None else total[k] + term
                for k in range(BLOCK):
                    out[first + k, s : s + 8, :] = jnp.zeros((8, hz), F32) if total[k] is None else total[k]

    def along_z(v, y):
        at = pl.ds(pl.multiple_of(v * width, width), width)
        high, low = split(y[pl.ds(lead, wy)].reshape(wy * width, hz))
        out = mul(jnp.concatenate([high, low, high], axis=1), kz[v]).reshape(wy, width, 2 * hz)
        gm[:, at, :] = out[..., :hz]
        for o in range(2 * rims):
            total = out[o * group, :, hz:]
            for m in range(1, group):
                total = total + pltpu.roll(out[o * group + m, :, hz:], rad * m, 1)
            gh[o, at, :] = total

    along_y(0, ya)

    def views(p, carry):
        along_y(2 * p + 1, yb)
        along_z(2 * p, ya)
        along_y(jnp.minimum(2 * p + 2, nviews - 1), ya)
        along_z(2 * p + 1, yb)
        return carry

    lax.fori_loop(0, nviews // 2, views, 0)

    def store(out, row):
        for c, ref in enumerate((kept, sent)):
            for k in range(ref.shape[0]):
                first = (c * ref.shape[0] + k) * width
                ref[k, row] = out[first : first + width]

    for c in range(2):
        for k in range(rims):
            store(mul(wxt[...], stack3(gh[c * rims + k])), c * (half + rims) + half + k)

        for y in range(c * half, (c + 1) * half, 2):
            out = mul(wxt[...], stack3(jnp.concatenate([gm[y], gm[y + 1]], axis=1)))
            store(out[:, :hz], c * rims + y)
            store(out[:, hz:], c * rims + y + 1)


def row_of(a, b, y, half):
    return a[y] if y < half else b[y - half]


def pack_kernel(rad, place, a, b, to_y, to_z, to_c, edge):
    yh, zh = place[0], place[1]
    rows, width, hz = a.shape
    group = hz // rad
    half = rows * group // (group + 1)
    rims, wy = half // group, 2 * half
    begin = (hz - rad) * (1 - zh)
    lane = lane_of((width, hz)) // rad
    for o in range(2 * rims):
        total = None
        for m in range(group):
            value = pltpu.roll(row_of(a, b, o * group + m, half), (rad * m - begin + hz) % hz, 1)
            total = value if m == 0 else jnp.where(lane == m, value, total)
        edge[o] = total
        to_z[2 * rims + o] = total
        to_z[o] = (a if o < rims else b)[half + o % rims]
    hy = wy - rad
    over = hy // group
    for y in range(wy):
        @pl.when(jnp.logical_and(y >= rad * (1 - yh), y < rad * (1 - yh) + hy))
        def _():
            to_y[y - rad * (1 - yh)] = row_of(a, b, y, half)
    skip = (rad // group) * (1 - yh)
    for k in range(over):
        to_y[hy + k] = to_z[skip + k]
        to_c[k] = to_z[skip + k]
        to_c[over + k] = edge[skip + k]


def update_kernel(rad, place, a, b, fy, fz, fc, old, count, new):
    yh, zh = place[0], place[1]
    rows, width, hz = a.shape
    group = hz // rad
    half = rows * group // (group + 1)
    rims, wy = half // group, 2 * half
    hy = wy - rad
    over = hy // group
    start, skip = rad * (1 - yh), (rad // group) * (1 - yh)
    begin = (hz - rad) * (1 - zh)
    zero = jnp.zeros((width, hz), F32)
    inside = (lane_of((width, hz)) >= begin) & (lane_of((width, hz)) < begin + rad)
    total = count[...]

    def part(ref, first, at, limit):
        ok = jnp.logical_and(at >= 0, at < limit)
        return jnp.where(ok, ref[first + jnp.clip(at, 0, limit - 1)], zero)

    for o in range(2 * rims):
        h, k = o // rims, o % rims
        row = h * rows + half + k
        rim = (a, b)[h][half + k] + fz[2 * rims + o]
        rim = rim + part(fy, hy, o - skip, over) + part(fc, over, o - skip, over)
        new[row] = old[row] * rim / total
        edge = fz[o] + part(fc, 0, o - skip, over)
        for m in range(group):
            y = o * group + m
            moved = jnp.where(inside, pltpu.roll(edge, (begin - rad * m + hz) % hz, 1), 0.0)
            value = row_of(a, b, y, half) + part(fy, 0, y - start, hy) + moved
            row = h * rows + y - h * half
            new[row] = old[row] * value / total


def assemble_kernel(where, *refs):
    pieces, out = refs[:-1], refs[-1]
    hy, width, hz = pieces[0].shape
    for r, piece in enumerate(pieces):
        for owner in range(len(pieces)):
            oz, oy = owner >> 1, (owner ^ (owner >> 1)) & 1

            @pl.when(where[0] == owner ^ r)
            def _():
                for y in range(hy):
                    out[:, oy * hy + y, oz * hz : (oz + 1) * hz] = piece[y]


VMEM = pl.BlockSpec(memory_space=pltpu.VMEM)
ANY = pl.BlockSpec(memory_space=pl.ANY)
SMEM = pl.BlockSpec(memory_space=pltpu.SMEM)


def call(kernel, shapes, scratch, smem, cost, *args, late=()):
    flops, moved = cost
    return pl.pallas_call(
        kernel,
        out_shape=[jax.ShapeDtypeStruct(shape, F32) for shape in shapes],
        in_specs=[SMEM] * smem + [VMEM] * (len(args) - smem) + [ANY] * len(late),
        out_specs=[VMEM] * len(shapes),
        scratch_shapes=[pltpu.VMEM(s, F32) if isinstance(s, tuple) else s for s in scratch],
        compiler_params=PARAMS,
        cost_estimate=pl.CostEstimate(flops=flops, bytes_accessed=moved, transcendentals=0),
    )(*args, *late)


def body(prior, data, taps, offsets, coverage):
    nview, nspace = lax.axis_size("view"), lax.axis_size("space")
    g, j = lax.axis_index("view"), lax.axis_index("space")
    zh, yh = g >> 1, (g ^ (g >> 1)) & 1
    place_yz = jnp.stack([yh, zh]).astype(jnp.int32)
    local, width, ny, nz = data.shape
    ntaps = taps.shape[-1]
    rad = ntaps // 2
    hy, hz = ny // 2, nz // 2
    wy = hy + rad
    group = hz // rad
    half, rims = wy // 2, wy // 2 // group
    rows = half + rims

    flat = jnp.concatenate(
        [
            taps.reshape(local, -1),
            offsets.astype(jnp.float32)[:, None],
            coverage.astype(jnp.float32),
        ],
        axis=1,
    )
    used = flat.shape[1]
    flat = jnp.pad(flat, ((0, 0), (0, -used % LANES)))
    shared = [flat] + [swap(flat, "view", r) for r in range(1, nview)]
    shared = jnp.concatenate(shared, axis=0)

    def quadrant(owner):
        oz, oy = owner >> 1, (owner ^ (owner >> 1)) & 1
        return lax.dynamic_slice(data, (0, 0, oy * hy, oz * hz), (local, width, hy, hz))

    pieces = [quadrant(g)] + [swap(quadrant(g ^ r), "view", r) for r in range(1, nview)]

    nviews = nview * local
    nvi = nviews * width
    kern = shared[:, : 3 * ntaps].reshape(nviews, 3, ntaps)
    kern = kern / jnp.sum(kern, axis=-1, keepdims=True)
    turn = shared[:, 3 * ntaps].astype(jnp.int32)
    cover = shared[:, 3 * ntaps + 1 : used]
    count = jnp.broadcast_to(jnp.sum(cover, axis=0)[:, None], (width, hz))
    note = jnp.pad(cover.T, ((0, 0), (0, hz - nviews)))[None]

    window = lax.dynamic_slice_in_dim(prior, rad * yh, wy, axis=1).transpose(1, 0, 2)
    main = lax.dynamic_slice_in_dim(window, hz * zh, hz, axis=2)
    rim = lax.dynamic_slice_in_dim(window, jnp.where(zh == 0, hz, hz - rad), rad, axis=2)
    rim = rim.reshape(2 * rims, group, width, rad).transpose(0, 2, 1, 3).reshape(2 * rims, width, hz)
    parts = [main[:half], rim[:rims], main[half:], rim[rims:]]
    estimate = jnp.concatenate(parts, axis=0)
    wide = gather([jnp.concatenate(parts[:2], axis=0), jnp.concatenate(parts[2:], axis=0)])
    cover = jnp.concatenate(gather([note]), axis=1)[..., :nviews]
    cover = cover.transpose(3, 1, 0, 2).reshape(nviews, 1, nspace * width)

    slab = (j - turn) % nspace
    spot = slab[:, None] * width + jnp.arange(width)
    order = jnp.arange(nspace).reshape(nspace // 2, 2).T.reshape(-1)
    planes = ((j ^ order)[:, None] * width + jnp.arange(width)).reshape(-1)
    band_x = pick(kern[:, 0], planes - spot[:, :, None] + rad)
    band_xt = (band_x * cover).reshape(nvi, -1).T
    band_x = band_x.reshape(nvi, -1)

    def halves(value):
        high = lax.reduce_precision(value, 8, 7)
        return high.astype(BF16), (value - high).astype(BF16)

    def triple(value):
        high, low = halves(value)
        return jnp.concatenate([high, high, low], axis=1)

    wx, wxt = triple(band_x), triple(band_xt)
    cells = jnp.concatenate([jnp.arange(hz) + hz * zh, jnp.arange(hz) + jnp.where(zh == 0, hz, hz - rad)])
    real = jnp.arange(2 * hz) < hz + rad
    goal = jnp.arange(hz) + hz * zh
    index = jnp.where(real[:, None], cells[:, None] - goal + rad, -1)
    band_z = pick(kern[:, 2], index[None])
    high, low = halves(band_z)
    kz = [high[:, :hz], high[:, :hz], low[:, :hz]]
    kz += [high[:, hz : hz + rad], high[:, hz : hz + rad], low[:, hz : hz + rad]]
    kz = jnp.concatenate(kz + [jnp.zeros((nviews, hz - 3 * rad, hz), BF16)], axis=1)
    high, low = halves(band_z.transpose(0, 2, 1))
    kzt = jnp.concatenate([high, high, low], axis=1)
    ky = kern[:, 1]

    plane = width * hz
    mxu = 2 * 3 * nvi * plane * 2 * rows * (nspace // 2)

    def ahead(wide, late, cost):
        return call(
            functools.partial(ahead_kernel, rad),
            [(hy, nvi, hz)],
            [(wy, nvi, hz), pltpu.VMEM((wy, nvi, hz), BF16), (wy + rad, width, hz), (wy + rad, width, hz)],
            2,
            cost,
            place_yz, ky, wx, kz, *wide,
            late=late,
        )[0]

    def back(blurred):
        return call(
            functools.partial(back_kernel, rad, nview),
            [(nspace // 2, 2 * rows, width, hz)] * 2,
            [(hy, nvi, hz), (hy + 2 * rad, width, hz), (hy + 2 * rad, width, hz), (wy, nvi, hz), (2 * rims, nvi, hz)],
            2,
            (mxu, 4 * plane * (nspace * 2 * rows + 2 * hy * nviews)),
            place_yz, ky, wxt, kzt, blurred, *pieces,
        )

    over = hy // group
    for step in range(ITERS):
        if step:
            wide = gather([estimate[:rows], estimate[rows:]])
        blurred = ahead(wide, () if step else tuple(pieces[1:3]), (mxu if step else 0, plane))
        a, b = scatter_sum(*back(blurred))
        to_y, to_z, to_c = call(
            functools.partial(pack_kernel, rad),
            [(hy + over, width, hz), (4 * rims, width, hz), (2 * over, width, hz)],
            [(2 * rims, width, hz)],
            1,
            (plane, 4 * plane * 4 * rows),
            place_yz, a, b,
        )
        estimate = call(
            functools.partial(update_kernel, rad),
            [(2 * rows, width, hz)],
            [],
            1,
            (plane, 4 * plane * 8 * rows),
            place_yz, a, b, swap(to_y, "view", 1), swap(to_z, "view", 3), swap(to_c, "view", 2), estimate, count,
        )[0]

    main = jnp.concatenate([estimate[:half], estimate[rows : rows + half]], axis=0)
    own = lax.dynamic_slice_in_dim(main, rad * yh, hy, axis=0)
    parts = [own] + [swap(own, "view", r) for r in range(1, nview)]
    return call(
        assemble_kernel,
        [(width, ny, nz)],
        [],
        1,
        (plane, 16 * plane * ny),
        g.astype(jnp.int32)[None], *parts,
    )[0]


def solution(mesh):
    return jax.shard_map(
        body,
        mesh=mesh,
        in_specs=(
            P("space", None, None),
            P("view", "space", None, None),
            P("view", None, None),
            P("view"),
            P("view", "space"),
        ),
        out_specs=P("space", None, None),
        check_vma=False,
    )
```

```python
import functools

import jax
import jax.numpy as jnp
from jax import lax
from jax.experimental import pallas as pl
from jax.experimental.pallas import tpu as pltpu
from jax.sharding import PartitionSpec as P

ITERS = 2
LANES = 128
BLOCK = 8
F32, BF16 = jnp.float32, jnp.bfloat16
PARAMS = pltpu.CompilerParams(vmem_limit_bytes=58 * 1024 * 1024)


def swap(value, axis, mask):
    count = lax.axis_size(axis)
    return lax.ppermute(value, axis, [(i, i ^ mask) for i in range(count)])


def orders(bits):
    shift = (bits - 1) // 2
    upper = list(range(1, bits))
    return upper, upper[shift:] + upper[:shift]


def scatter_sum(kept, sent):
    bits = lax.axis_size("space").bit_length() - 1
    blocks = kept + swap(sent, "space", 1)
    middle = blocks.shape[1] // 2
    out = []
    for part, order in zip((blocks[:, :middle], blocks[:, middle:]), orders(bits)):
        left = list(range(1, bits))
        for bit in order:
            low = 1 << left.index(bit)
            split = part.reshape((part.shape[0] // (2 * low), 2, low) + part.shape[1:])
            part = split[:, 0] + swap(split[:, 1], "space", 1 << bit)
            part = part.reshape((-1,) + part.shape[2:])
            left.remove(bit)
        out.append(part[0])
    return out


def gather(parts):
    bits = lax.axis_size("space").bit_length() - 1
    out = []
    for part, order in zip(parts, orders(bits)):
        part = part[None]
        have = []
        for bit in reversed(order):
            low = 1 << sum(other < bit for other in have)
            part = part.reshape((part.shape[0] // low, 1, low) + part.shape[1:])
            part = jnp.concatenate([part, swap(part, "space", 1 << bit)], axis=1)
            part = part.reshape((-1,) + part.shape[3:])
            have.append(bit)
        out += [part, swap(part, "space", 1)]
    return out


def split(value):
    high = value.astype(BF16)
    return high, (value - high.astype(F32)).astype(BF16)


def stack3(value):
    high, low = split(value)
    return jnp.concatenate([high, low, high], axis=0)


def mul(a, b):
    return jnp.dot(a, b, preferred_element_type=F32)


def lane_of(shape):
    return lax.broadcasted_iota(jnp.int32, shape, len(shape) - 1)


def bands_kernel(rad, place, slab, kern, wx, bxt, kz, kzt):
    zh, j = place[1], place[2]
    nx, nvi = bxt.shape
    nviews, _, hz = kz.shape
    width = nvi // nviews
    taps = 2 * rad

    def taken(v, axis, index):
        total = jnp.zeros(index.shape, F32)
        for t in range(taps):
            total = jnp.where(index == t, kern[v, axis * taps + t], total)
        return total

    shape = (width, nx)
    lane, row = lane_of(shape), lax.broadcasted_iota(jnp.int32, shape, 0)
    block = lane // width
    blocks = nx // width // 2
    block = jnp.bitwise_xor(2 * (block % blocks) + block // blocks, jnp.full(shape, j, jnp.int32))
    cell = block * width + lane % width - row + rad
    for v in range(nviews):
        value = taken(v, 0, cell - slab[v] * width)
        high, low = split(value)
        at = pl.ds(v * width, width)
        wx[at, :nx] = high
        wx[at, nx : 2 * nx] = high
        wx[at, 2 * nx :] = low
        bxt[:, v * width : (v + 1) * width] = value.T
    shape = (hz, hz)
    middle = lax.broadcasted_iota(jnp.int32, shape, 0) - lane_of(shape) + rad
    shape = (rad, hz)
    outer = lax.broadcasted_iota(jnp.int32, shape, 0) - lane_of(shape) + (hz + rad) * (1 - zh)

    def one(v, carry):
        main, rim = taken(v, 2, middle), taken(v, 2, outer)
        high, low = split(main)
        rim_high, rim_low = split(rim)
        rest = jnp.zeros((hz - 3 * rad, hz), BF16)
        kz[v] = jnp.concatenate([high, high, low, rim_high, rim_high, rim_low, rest], axis=0)
        rim = jnp.concatenate([rim, jnp.zeros((hz - rad, hz), F32)], axis=0)
        high, low = split(jnp.concatenate([main.T, rim.T], axis=1))
        kzt[v] = jnp.concatenate([high, high, low], axis=0)
        return carry

    lax.fori_loop(0, nviews, one, 0)


def ahead_kernel(rad, place, ky, wx, kz, a0, a1, b0, b1, *refs):
    blurred, u, uh, za, zb = refs[-5:]
    yh = place[0]
    wy, nvi, hz = u.shape
    hy = blurred.shape[0]
    width = a0.shape[2]
    nviews = nvi // width
    half, group = wy // 2, hz // rad
    part = lane_of((nvi, hz)) // rad
    for h, pair in enumerate(((a0, a1), (b0, b1))):

        def row(y):
            return jnp.concatenate([ref[k, y] for ref in pair for k in range(ref.shape[0])], axis=0)

        for k in range(half // group):
            out = mul(wx[...], stack3(row(half + k)))
            high = out.astype(BF16).astype(F32)
            low = out - high
            for m in range(group):
                first, second, third = (
                    pltpu.roll(value, (rad * (at - m)) % hz, 1) if at != m else value
                    for at, value in enumerate((high, low, high))
                )
                value = jnp.where(part == 0, first, jnp.where(part == 1, second, jnp.where(part == 2, third, 0.0)))
                uh[h * half + k * group + m] = value.astype(BF16)

        for y in range(0, half, 2):
            out = mul(wx[...], stack3(jnp.concatenate([row(y), row(y + 1)], axis=1)))
            u[h * half + y] = out[:, :hz]
            u[h * half + y + 1] = out[:, hz:]

    lead = rad * (1 - yh)
    for z in (za, zb):
        z[pl.ds(wy * yh, rad)] = jnp.zeros((rad, width, hz), F32)

    def along_z(v, z):
        at = pl.ds(pl.multiple_of(v * width, width), width)
        high, low = split(u[:, at, :].reshape(wy * width, hz))
        value = jnp.concatenate([high, low, high, uh[:, at, :].reshape(wy * width, hz)], axis=1)
        z[pl.ds(lead, wy)] = mul(value, kz[v]).reshape(wy, width, hz)

    def along_y(v, z):
        tap = [ky[v, t] for t in range(2 * rad)]
        for s in range(0, width, 8):
            for first in range(0, hy, BLOCK):
                total = [None] * BLOCK
                for y in range(first, first + BLOCK + 2 * rad - 1):
                    value = z[y, s : s + 8, :]
                    for k in range(BLOCK):
                        t = y - first - k
                        if 0 <= t < 2 * rad:
                            term = tap[t] * value
                            total[k] = term if total[k] is None else total[k] + term
                for k in range(BLOCK):
                    blurred[first + k, pl.ds(pl.multiple_of(v * width + s, 8), 8), :] = total[k]

    along_z(0, za)

    def views(p, carry):
        along_z(2 * p + 1, zb)
        along_y(2 * p, za)
        along_z(jnp.minimum(2 * p + 2, nviews - 1), za)
        along_y(2 * p + 1, zb)
        return carry

    lax.fori_loop(0, nviews // 2, views, 0)


def back_kernel(rad, npieces, place, ky, bxt, note0, note1, kz, blurred, *refs):
    pieces, (kept, sent, r, ya, yb, gm, gh, wxt) = refs[:npieces], refs[npieces:]
    yh = place[0]
    hy, nvi, hz = blurred.shape
    wy = gm.shape[0]
    local, width = pieces[0].shape[:2]
    nviews = nvi // width
    half, group = wy // 2, hz // rad
    rims = half // group
    cover = jnp.concatenate([ref[k, 0] for ref in (note0, note1) for k in range(ref.shape[0])], axis=0)
    shape = (hz, nvi)
    spread = jnp.where(lane_of(shape) // width == lax.broadcasted_iota(jnp.int32, shape, 0), 1.0, 0.0)
    high, low = split(bxt[...] * mul(cover.astype(BF16), spread.astype(BF16)))
    wxt[...] = jnp.concatenate([high, high, low], axis=1)
    for p, piece in enumerate(pieces):
        for k in range(local):
            first = (p * local + k) * width
            for y in range(hy):
                r[y, first : first + width, :] = piece[k, :, y, :] / blurred[y, first : first + width, :]

    lead = rad * (1 - yh)

    def along_y(v, out):
        tap = [ky[v, t] for t in range(2 * rad)]
        for s in range(0, width, 8):
            at = pl.ds(pl.multiple_of(v * width + s, 8), 8)
            for first in range(0, hy + 2 * rad, BLOCK):
                total = [None] * BLOCK
                for y in range(max(0, first - 2 * rad + 1), min(hy, first + BLOCK)):
                    value = r[y, at, :]
                    for k in range(BLOCK):
                        t = first + k - y
                        if 0 <= t < 2 * rad:
                            term = tap[t] * value
                            total[k] = term if total[k] is None else total[k] + term
                for k in range(BLOCK):
                    out[first + k, s : s + 8, :] = jnp.zeros((8, hz), F32) if total[k] is None else total[k]

    def along_z(v, y):
        at = pl.ds(pl.multiple_of(v * width, width), width)
        high, low = split(y[pl.ds(lead, wy)].reshape(wy * width, hz))
        out = mul(jnp.concatenate([high, low, high], axis=1), kz[v]).reshape(wy, width, 2 * hz)
        gm[:, at, :] = out[..., :hz]
        for o in range(2 * rims):
            total = out[o * group, :, hz:]
            for m in range(1, group):
                total = total + pltpu.roll(out[o * group + m, :, hz:], rad * m, 1)
            gh[o, at, :] = total

    along_y(0, ya)

    def views(p, carry):
        along_y(2 * p + 1, yb)
        along_z(2 * p, ya)
        along_y(jnp.minimum(2 * p + 2, nviews - 1), ya)
        along_z(2 * p + 1, yb)
        return carry

    lax.fori_loop(0, nviews // 2, views, 0)

    def store(out, row):
        for c, ref in enumerate((kept, sent)):
            for k in range(ref.shape[0]):
                first = (c * ref.shape[0] + k) * width
                ref[k, row] = out[first : first + width]

    for c in range(2):
        for k in range(rims):
            store(mul(wxt[...], stack3(gh[c * rims + k])), c * (half + rims) + half + k)

        for y in range(c * half, (c + 1) * half, 2):
            out = mul(wxt[...], stack3(jnp.concatenate([gm[y], gm[y + 1]], axis=1)))
            store(out[:, :hz], c * rims + y)
            store(out[:, hz:], c * rims + y + 1)


def row_of(a, b, y, half):
    return a[y] if y < half else b[y - half]


def pack_kernel(rad, place, a, b, to_y, to_z, to_c, edge):
    yh, zh = place[0], place[1]
    rows, width, hz = a.shape
    group = hz // rad
    half = rows * group // (group + 1)
    rims, wy = half // group, 2 * half
    begin = (hz - rad) * (1 - zh)
    lane = lane_of((width, hz)) // rad
    for o in range(2 * rims):
        total = None
        for m in range(group):
            value = pltpu.roll(row_of(a, b, o * group + m, half), (rad * m - begin + hz) % hz, 1)
            total = value if m == 0 else jnp.where(lane == m, value, total)
        edge[o] = total
        to_z[2 * rims + o] = total
        to_z[o] = (a if o < rims else b)[half + o % rims]
    hy = wy - rad
    over = hy // group
    for y in range(wy):
        @pl.when(jnp.logical_and(y >= rad * (1 - yh), y < rad * (1 - yh) + hy))
        def _():
            to_y[y - rad * (1 - yh)] = row_of(a, b, y, half)
    skip = (rad // group) * (1 - yh)
    for k in range(over):
        to_y[hy + k] = to_z[skip + k]
        to_c[k] = to_z[skip + k]
        to_c[over + k] = edge[skip + k]


def update_kernel(rad, place, a, b, fy, fz, fc, old, count, new):
    yh, zh = place[0], place[1]
    rows, width, hz = a.shape
    group = hz // rad
    half = rows * group // (group + 1)
    rims, wy = half // group, 2 * half
    hy = wy - rad
    over = hy // group
    start, skip = rad * (1 - yh), (rad // group) * (1 - yh)
    begin = (hz - rad) * (1 - zh)
    zero = jnp.zeros((width, hz), F32)
    inside = (lane_of((width, hz)) >= begin) & (lane_of((width, hz)) < begin + rad)
    total = count[...]

    def part(ref, first, at, limit):
        ok = jnp.logical_and(at >= 0, at < limit)
        return jnp.where(ok, ref[first + jnp.clip(at, 0, limit - 1)], zero)

    for o in range(2 * rims):
        h, k = o // rims, o % rims
        row = h * rows + half + k
        rim = (a, b)[h][half + k] + fz[2 * rims + o]
        rim = rim + part(fy, hy, o - skip, over) + part(fc, over, o - skip, over)
        new[row] = old[row] * rim / total
        edge = fz[o] + part(fc, 0, o - skip, over)
        for m in range(group):
            y = o * group + m
            moved = jnp.where(inside, pltpu.roll(edge, (begin - rad * m + hz) % hz, 1), 0.0)
            value = row_of(a, b, y, half) + part(fy, 0, y - start, hy) + moved
            row = h * rows + y - h * half
            new[row] = old[row] * value / total


def assemble_kernel(where, *refs):
    pieces, out = refs[:-1], refs[-1]
    hy, width, hz = pieces[0].shape
    for r, piece in enumerate(pieces):
        for owner in range(len(pieces)):
            oz, oy = owner >> 1, (owner ^ (owner >> 1)) & 1

            @pl.when(where[0] == owner ^ r)
            def _():
                for y in range(hy):
                    out[:, oy * hy + y, oz * hz : (oz + 1) * hz] = piece[y]


VMEM = pl.BlockSpec(memory_space=pltpu.VMEM)
ANY = pl.BlockSpec(memory_space=pl.ANY)
SMEM = pl.BlockSpec(memory_space=pltpu.SMEM)


def call(kernel, shapes, scratch, smem, cost, *args, late=()):
    flops, moved = cost
    return pl.pallas_call(
        kernel,
        out_shape=[jax.ShapeDtypeStruct(shape, F32) for shape in shapes],
        in_specs=[SMEM] * smem + [VMEM] * (len(args) - smem) + [ANY] * len(late),
        out_specs=[VMEM] * len(shapes),
        scratch_shapes=[pltpu.VMEM(s, F32) if isinstance(s, tuple) else s for s in scratch],
        compiler_params=PARAMS,
        cost_estimate=pl.CostEstimate(flops=flops, bytes_accessed=moved, transcendentals=0),
    )(*args, *late)


def body(prior, data, taps, offsets, coverage):
    nview, nspace = lax.axis_size("view"), lax.axis_size("space")
    g, j = lax.axis_index("view"), lax.axis_index("space")
    zh, yh = g >> 1, (g ^ (g >> 1)) & 1
    place_yz = jnp.stack([yh, zh, j]).astype(jnp.int32)
    local, width, ny, nz = data.shape
    ntaps = taps.shape[-1]
    rad = ntaps // 2
    hy, hz = ny // 2, nz // 2
    wy = hy + rad
    group = hz // rad
    half, rims = wy // 2, wy // 2 // group
    rows = half + rims

    flat = jnp.concatenate(
        [
            taps.reshape(local, -1),
            offsets.astype(jnp.float32)[:, None],
            coverage.astype(jnp.float32),
        ],
        axis=1,
    )
    used = flat.shape[1]
    flat = jnp.pad(flat, ((0, 0), (0, -used % LANES)))
    shared = [flat] + [swap(flat, "view", r) for r in range(1, nview)]
    shared = jnp.concatenate(shared, axis=0)

    def quadrant(owner):
        oz, oy = owner >> 1, (owner ^ (owner >> 1)) & 1
        return lax.dynamic_slice(data, (0, 0, oy * hy, oz * hz), (local, width, hy, hz))

    pieces = [quadrant(g)] + [swap(quadrant(g ^ r), "view", r) for r in range(1, nview)]

    nviews = nview * local
    nvi = nviews * width
    kern = shared[:, : 3 * ntaps].reshape(nviews, 3, ntaps)
    kern = kern / jnp.sum(kern, axis=-1, keepdims=True)
    turn = shared[:, 3 * ntaps].astype(jnp.int32)
    cover = shared[:, 3 * ntaps + 1 : used]
    count = jnp.broadcast_to(jnp.sum(cover, axis=0)[:, None], (width, hz))
    note = jnp.pad(cover.T, ((0, 0), (0, hz - nviews)))[None]

    window = lax.dynamic_slice_in_dim(prior, rad * yh, wy, axis=1).transpose(1, 0, 2)
    main = lax.dynamic_slice_in_dim(window, hz * zh, hz, axis=2)
    rim = lax.dynamic_slice_in_dim(window, jnp.where(zh == 0, hz, hz - rad), rad, axis=2)
    rim = rim.reshape(2 * rims, group, width, rad).transpose(0, 2, 1, 3).reshape(2 * rims, width, hz)
    parts = [main[:half], rim[:rims], main[half:], rim[rims:]]
    estimate = jnp.concatenate(parts, axis=0)
    wide = gather([jnp.concatenate(parts[:2], axis=0), jnp.concatenate(parts[2:], axis=0)])
    notes = gather([note])

    nx = nspace * width
    wx, bxt, kz, kzt = pl.pallas_call(
        functools.partial(bands_kernel, rad),
        out_shape=[
            jax.ShapeDtypeStruct((nvi, 3 * nx), BF16),
            jax.ShapeDtypeStruct((nx, nvi), F32),
            jax.ShapeDtypeStruct((nviews, 4 * hz, hz), BF16),
            jax.ShapeDtypeStruct((nviews, 3 * hz, 2 * hz), BF16),
        ],
        in_specs=[SMEM] * 3,
        out_specs=[VMEM] * 4,
        compiler_params=PARAMS,
        cost_estimate=pl.CostEstimate(flops=nviews * hz * hz * 32, bytes_accessed=nviews * hz * hz * 16, transcendentals=0),
    )(place_yz, (j - turn) % nspace, kern.reshape(nviews, -1))
    ky = kern[:, 1]

    plane = width * hz
    mxu = 2 * 3 * nvi * plane * 2 * rows * (nspace // 2)

    def ahead(wide, late, cost):
        return call(
            functools.partial(ahead_kernel, rad),
            [(hy, nvi, hz)],
            [(wy, nvi, hz), pltpu.VMEM((wy, nvi, hz), BF16), (wy + rad, width, hz), (wy + rad, width, hz)],
            2,
            cost,
            place_yz, ky, wx, kz, *wide,
            late=late,
        )[0]

    def back(blurred):
        return call(
            functools.partial(back_kernel, rad, nview),
            [(nspace // 2, 2 * rows, width, hz)] * 2,
            [(hy, nvi, hz), (hy + 2 * rad, width, hz), (hy + 2 * rad, width, hz), (wy, nvi, hz), (2 * rims, nvi, hz), pltpu.VMEM((nx, 3 * nvi), BF16)],
            2,
            (mxu, 4 * plane * (nspace * 2 * rows + 2 * hy * nviews)),
            place_yz, ky, bxt, *notes, kzt, blurred, *pieces,
        )

    over = hy // group
    for step in range(ITERS):
        if step:
            wide = gather([estimate[:rows], estimate[rows:]])
        blurred = ahead(wide, () if step else tuple(pieces[1:3]), (mxu if step else 0, plane))
        a, b = scatter_sum(*back(blurred))
        to_y, to_z, to_c = call(
            functools.partial(pack_kernel, rad),
            [(hy + over, width, hz), (4 * rims, width, hz), (2 * over, width, hz)],
            [(2 * rims, width, hz)],
            1,
            (plane, 4 * plane * 4 * rows),
            place_yz, a, b,
        )
        estimate = call(
            functools.partial(update_kernel, rad),
            [(2 * rows, width, hz)],
            [],
            1,
            (plane, 4 * plane * 8 * rows),
            place_yz, a, b, swap(to_y, "view", 1), swap(to_z, "view", 3), swap(to_c, "view", 2), estimate, count,
        )[0]

    main = jnp.concatenate([estimate[:half], estimate[rows : rows + half]], axis=0)
    own = lax.dynamic_slice_in_dim(main, rad * yh, hy, axis=0)
    parts = [own] + [swap(own, "view", r) for r in range(1, nview)]
    return call(
        assemble_kernel,
        [(width, ny, nz)],
        [],
        1,
        (plane, 16 * plane * ny),
        g.astype(jnp.int32)[None], *parts,
    )[0]


def solution(mesh):
    return jax.shard_map(
        body,
        mesh=mesh,
        in_specs=(
            P("space", None, None),
            P("view", "space", None, None),
            P("view", None, None),
            P("view"),
            P("view", "space"),
        ),
        out_specs=P("space", None, None),
        check_vma=False,
    )
```

```python
import functools

import jax
import jax.numpy as jnp
from jax import lax
from jax.experimental import pallas as pl
from jax.experimental.pallas import tpu as pltpu
from jax.sharding import PartitionSpec as P

ITERS = 2
LANES = 128
BLOCK = 8
F32, BF16 = jnp.float32, jnp.bfloat16
PARAMS = pltpu.CompilerParams(vmem_limit_bytes=58 * 1024 * 1024)


def swap(value, axis, mask):
    count = lax.axis_size(axis)
    return lax.ppermute(value, axis, [(i, i ^ mask) for i in range(count)])


def orders(bits):
    shift = (bits - 1) // 2
    upper = list(range(1, bits))
    return upper, upper[shift:] + upper[:shift]


def scatter_sum(kept, sent):
    bits = lax.axis_size("space").bit_length() - 1
    blocks = kept + swap(sent, "space", 1)
    middle = blocks.shape[1] // 2
    out = []
    for part, order in zip((blocks[:, :middle], blocks[:, middle:]), orders(bits)):
        left = list(range(1, bits))
        for bit in order:
            low = 1 << left.index(bit)
            split = part.reshape((part.shape[0] // (2 * low), 2, low) + part.shape[1:])
            part = split[:, 0] + swap(split[:, 1], "space", 1 << bit)
            part = part.reshape((-1,) + part.shape[2:])
            left.remove(bit)
        out.append(part[0])
    return out


def gather(parts):
    bits = lax.axis_size("space").bit_length() - 1
    out = []
    for part, order in zip(parts, orders(bits)):
        part = part[None]
        have = []
        for bit in reversed(order):
            low = 1 << sum(other < bit for other in have)
            part = part.reshape((part.shape[0] // low, 1, low) + part.shape[1:])
            part = jnp.concatenate([part, swap(part, "space", 1 << bit)], axis=1)
            part = part.reshape((-1,) + part.shape[3:])
            have.append(bit)
        out += [part, swap(part, "space", 1)]
    return out


def split(value):
    high = value.astype(BF16)
    return high, (value - high.astype(F32)).astype(BF16)


def stack3(value):
    high, low = split(value)
    return jnp.concatenate([high, low, high], axis=0)


def mul(a, b):
    return jnp.dot(a, b, preferred_element_type=F32)


def lane_of(shape):
    return lax.broadcasted_iota(jnp.int32, shape, len(shape) - 1)


def bands_kernel(rad, place, slab, kern, wx, bxt, kz, kzt):
    zh, j = place[1], place[2]
    nx, nvi = bxt.shape
    nviews, _, hz = kz.shape
    width = nvi // nviews
    taps = 2 * rad

    def taken(v, axis, index):
        total = jnp.zeros(index.shape, F32)
        for t in range(taps):
            total = jnp.where(index == t, kern[v, axis * taps + t], total)
        return total

    shape = (width, nx)
    lane, row = lane_of(shape), lax.broadcasted_iota(jnp.int32, shape, 0)
    block = lane // width
    blocks = nx // width // 2
    block = jnp.bitwise_xor(2 * (block % blocks) + block // blocks, jnp.full(shape, j, jnp.int32))
    cell = block * width + lane % width - row + rad
    for v in range(nviews):
        value = taken(v, 0, cell - slab[v] * width)
        high, low = split(value)
        at = pl.ds(v * width, width)
        wx[at, :nx] = high
        wx[at, nx : 2 * nx] = high
        wx[at, 2 * nx :] = low
        bxt[:, v * width : (v + 1) * width] = value.T
    shape = (hz, hz)
    middle = lax.broadcasted_iota(jnp.int32, shape, 0) - lane_of(shape) + rad
    shape = (rad, hz)
    outer = lax.broadcasted_iota(jnp.int32, shape, 0) - lane_of(shape) + (hz + rad) * (1 - zh)

    def one(v, carry):
        main, rim = taken(v, 2, middle), taken(v, 2, outer)
        high, low = split(main)
        rim_high, rim_low = split(rim)
        rest = jnp.zeros((hz - 3 * rad, hz), BF16)
        kz[v] = jnp.concatenate([high, high, low, rim_high, rim_high, rim_low, rest], axis=0)
        rim = jnp.concatenate([rim, jnp.zeros((hz - rad, hz), F32)], axis=0)
        high, low = split(jnp.concatenate([main.T, rim.T], axis=1))
        kzt[v] = jnp.concatenate([high, high, low], axis=0)
        return carry

    lax.fori_loop(0, nviews, one, 0)


def ahead_kernel(rad, place, ky, wx, kz, a0, a1, b0, b1, *refs):
    blurred, u, uh, za, zb = refs[-5:]
    yh = place[0]
    wy, nvi, hz = u.shape
    hy = blurred.shape[0]
    width = a0.shape[2]
    nviews = nvi // width
    half, group = wy // 2, hz // rad
    part = lane_of((nvi, hz)) // rad
    for h, pair in enumerate(((a0, a1), (b0, b1))):

        def row(y):
            return jnp.concatenate([ref[k, y] for ref in pair for k in range(ref.shape[0])], axis=0)

        for k in range(half // group):
            out = mul(wx[...], stack3(row(half + k)))
            high = out.astype(BF16).astype(F32)
            low = out - high
            for m in range(group):
                first, second, third = (
                    pltpu.roll(value, (rad * (at - m)) % hz, 1) if at != m else value
                    for at, value in enumerate((high, low, high))
                )
                value = jnp.where(part == 0, first, jnp.where(part == 1, second, jnp.where(part == 2, third, 0.0)))
                uh[h * half + k * group + m] = value.astype(BF16)

        for y in range(0, half, 2):
            out = mul(wx[...], stack3(jnp.concatenate([row(y), row(y + 1)], axis=1)))
            u[h * half + y] = out[:, :hz]
            u[h * half + y + 1] = out[:, hz:]

    lead = rad * (1 - yh)
    for z in (za, zb):
        z[pl.ds(wy * yh, rad)] = jnp.zeros((rad, width, hz), F32)

    def along_z(v, z):
        at = pl.ds(pl.multiple_of(v * width, width), width)
        high, low = split(u[:, at, :].reshape(wy * width, hz))
        value = jnp.concatenate([high, low, high, uh[:, at, :].reshape(wy * width, hz)], axis=1)
        z[pl.ds(lead, wy)] = mul(value, kz[v]).reshape(wy, width, hz)

    def along_y(v, z):
        tap = [ky[v, t] for t in range(2 * rad)]
        for s in range(0, width, 8):
            for first in range(0, hy, BLOCK):
                total = [None] * BLOCK
                for y in range(first, first + BLOCK + 2 * rad - 1):
                    value = z[y, s : s + 8, :]
                    for k in range(BLOCK):
                        t = y - first - k
                        if 0 <= t < 2 * rad:
                            term = tap[t] * value
                            total[k] = term if total[k] is None else total[k] + term
                for k in range(BLOCK):
                    blurred[first + k, pl.ds(pl.multiple_of(v * width + s, 8), 8), :] = total[k]

    along_z(0, za)

    def views(p, carry):
        along_z(2 * p + 1, zb)
        along_y(2 * p, za)
        along_z(jnp.minimum(2 * p + 2, nviews - 1), za)
        along_y(2 * p + 1, zb)
        return carry

    lax.fori_loop(0, nviews // 2, views, 0)


def back_kernel(rad, npieces, place, ky, bxt, note0, note1, kz, blurred, *refs):
    pieces, (kept, sent, r, ya, yb, gm, gh, wxt) = refs[:npieces], refs[npieces:]
    yh = place[0]
    hy, nvi, hz = blurred.shape
    wy = gm.shape[0]
    local, width = pieces[0].shape[:2]
    nviews = nvi // width
    half, group = wy // 2, hz // rad
    rims = half // group
    cover = jnp.concatenate([ref[k, 0] for ref in (note0, note1) for k in range(ref.shape[0])], axis=0)
    shape = (hz, nvi)
    spread = jnp.where(lane_of(shape) // width == lax.broadcasted_iota(jnp.int32, shape, 0), 1.0, 0.0)
    high, low = split(bxt[...] * mul(cover.astype(BF16), spread.astype(BF16)))
    wxt[...] = jnp.concatenate([high, high, low], axis=1)
    for p, piece in enumerate(pieces):
        for k in range(local):
            first = (p * local + k) * width
            for y in range(hy):
                r[y, first : first + width, :] = piece[k, :, y, :] / blurred[y, first : first + width, :]

    lead = rad * (1 - yh)

    def along_y(v, out):
        tap = [ky[v, t] for t in range(2 * rad)]
        for s in range(0, width, 8):
            at = pl.ds(pl.multiple_of(v * width + s, 8), 8)
            for first in range(0, hy + 2 * rad, BLOCK):
                total = [None] * BLOCK
                for y in range(max(0, first - 2 * rad + 1), min(hy, first + BLOCK)):
                    value = r[y, at, :]
                    for k in range(BLOCK):
                        t = first + k - y
                        if 0 <= t < 2 * rad:
                            term = tap[t] * value
                            total[k] = term if total[k] is None else total[k] + term
                for k in range(BLOCK):
                    out[first + k, s : s + 8, :] = jnp.zeros((8, hz), F32) if total[k] is None else total[k]

    def along_z(v, y):
        at = pl.ds(pl.multiple_of(v * width, width), width)
        high, low = split(y[pl.ds(lead, wy)].reshape(wy * width, hz))
        out = mul(jnp.concatenate([high, low, high], axis=1), kz[v]).reshape(wy, width, 2 * hz)
        gm[:, at, :] = out[..., :hz]
        for o in range(2 * rims):
            total = out[o * group, :, hz:]
            for m in range(1, group):
                total = total + pltpu.roll(out[o * group + m, :, hz:], rad * m, 1)
            gh[o, at, :] = total

    along_y(0, ya)

    def views(p, carry):
        along_y(2 * p + 1, yb)
        along_z(2 * p, ya)
        along_y(jnp.minimum(2 * p + 2, nviews - 1), ya)
        along_z(2 * p + 1, yb)
        return carry

    lax.fori_loop(0, nviews // 2, views, 0)

    def store(out, row):
        for c, ref in enumerate((kept, sent)):
            for k in range(ref.shape[0]):
                first = (c * ref.shape[0] + k) * width
                ref[k, row] = out[first : first + width]

    for c in range(2):
        for k in range(rims):
            store(mul(wxt[...], stack3(gh[c * rims + k])), c * (half + rims) + half + k)

        for y in range(c * half, (c + 1) * half, 2):
            out = mul(wxt[...], stack3(jnp.concatenate([gm[y], gm[y + 1]], axis=1)))
            store(out[:, :hz], c * rims + y)
            store(out[:, hz:], c * rims + y + 1)


def row_of(a, b, y, half):
    return a[y] if y < half else b[y - half]


def pack_kernel(rad, place, a, b, to_y, to_z, to_c, edge):
    yh, zh = place[0], place[1]
    rows, width, hz = a.shape
    group = hz // rad
    half = rows * group // (group + 1)
    rims, wy = half // group, 2 * half
    begin = (hz - rad) * (1 - zh)
    lane = lane_of((width, hz)) // rad
    for o in range(2 * rims):
        total = None
        for m in range(group):
            value = pltpu.roll(row_of(a, b, o * group + m, half), (rad * m - begin + hz) % hz, 1)
            total = value if m == 0 else jnp.where(lane == m, value, total)
        edge[o] = total
        to_z[2 * rims + o] = total
        to_z[o] = (a if o < rims else b)[half + o % rims]
    hy = wy - rad
    over = hy // group
    for y in range(wy):
        @pl.when(jnp.logical_and(y >= rad * (1 - yh), y < rad * (1 - yh) + hy))
        def _():
            to_y[y - rad * (1 - yh)] = row_of(a, b, y, half)
    skip = (rad // group) * (1 - yh)
    for k in range(over):
        to_y[hy + k] = to_z[skip + k]
        to_c[k] = to_z[skip + k]
        to_c[over + k] = edge[skip + k]


def update_kernel(rad, place, a, b, fy, fz, fc, old_a, old_b, count, new_a, new_b):
    yh, zh = place[0], place[1]
    rows, width, hz = a.shape
    group = hz // rad
    half = rows * group // (group + 1)
    rims, wy = half // group, 2 * half
    hy = wy - rad
    over = hy // group
    start, skip = rad * (1 - yh), (rad // group) * (1 - yh)
    begin = (hz - rad) * (1 - zh)
    zero = jnp.zeros((width, hz), F32)
    inside = (lane_of((width, hz)) >= begin) & (lane_of((width, hz)) < begin + rad)
    total = count[...]

    def part(ref, first, at, limit):
        ok = jnp.logical_and(at >= 0, at < limit)
        return jnp.where(ok, ref[first + jnp.clip(at, 0, limit - 1)], zero)

    for o in range(2 * rims):
        h, k = o // rims, o % rims
        old, new, row = (old_a, old_b)[h], (new_a, new_b)[h], half + k
        rim = (a, b)[h][half + k] + fz[2 * rims + o]
        rim = rim + part(fy, hy, o - skip, over) + part(fc, over, o - skip, over)
        new[row] = old[row] * rim / total
        edge = fz[o] + part(fc, 0, o - skip, over)
        for m in range(group):
            y = o * group + m
            moved = jnp.where(inside, pltpu.roll(edge, (begin - rad * m + hz) % hz, 1), 0.0)
            value = row_of(a, b, y, half) + part(fy, 0, y - start, hy) + moved
            row = y - h * half
            new[row] = old[row] * value / total


def last_pack_kernel(rad, place, a, b, to_y, to_z, to_c):
    rows, _, hz = a.shape
    group = hz // rad
    half = rows * group // (group + 1)
    rims, own = half // group, 2 * half - rad
    for side in range(2):

        @pl.when(place[0] == side)
        def _():
            outer = own * (1 - side)
            for k in range(rad):
                to_y[k] = row_of(a, b, outer + k, half)
            for ref, first in ((to_z, rad * side // group), (to_c, outer // group)):
                for k in range(ref.shape[0]):
                    o = first + k
                    ref[k] = (a if o < rims else b)[half + o % rims]


def last_update_kernel(rad, place, a, b, fy, fz, fc, old_a, old_b, count, new):
    rows, width, hz = a.shape
    group = hz // rad
    half = rows * group // (group + 1)
    own = new.shape[1]
    begin = (hz - rad) * (1 - place[1])
    inside = (lane_of((width, hz)) >= begin) & (lane_of((width, hz)) < begin + rad)
    total = count[...]
    for side in range(2):

        @pl.when(place[0] == side)
        def _():
            first = (own - rad) * (1 - side)
            for k in range(own):
                y = rad * side + k
                value, edge = row_of(a, b, y, half), fz[k // group]
                if first <= k < first + rad:
                    value = value + fy[k - first]
                    edge = edge + fc[(k - first) // group]
                moved = pltpu.roll(edge, (begin - rad * (k % group) + hz) % hz, 1)
                value = value + jnp.where(inside, moved, 0.0)
                new[:, k, :] = row_of(old_a, old_b, y, half) * value / total


def assemble_kernel(where, *refs):
    pieces, out = refs[:-1], refs[-1]
    _, hy, hz = pieces[0].shape
    for r, piece in enumerate(pieces):
        for owner in range(len(pieces)):
            oz, oy = owner >> 1, (owner ^ (owner >> 1)) & 1

            @pl.when(where[0] == owner ^ r)
            def _():
                out[:, oy * hy : (oy + 1) * hy, oz * hz : (oz + 1) * hz] = piece[...]


VMEM = pl.BlockSpec(memory_space=pltpu.VMEM)
ANY = pl.BlockSpec(memory_space=pl.ANY)
SMEM = pl.BlockSpec(memory_space=pltpu.SMEM)


def call(kernel, shapes, scratch, smem, cost, *args, late=()):
    flops, moved = cost
    return pl.pallas_call(
        kernel,
        out_shape=[jax.ShapeDtypeStruct(shape, F32) for shape in shapes],
        in_specs=[SMEM] * smem + [VMEM] * (len(args) - smem) + [ANY] * len(late),
        out_specs=[VMEM] * len(shapes),
        scratch_shapes=[pltpu.VMEM(s, F32) if isinstance(s, tuple) else s for s in scratch],
        compiler_params=PARAMS,
        cost_estimate=pl.CostEstimate(flops=flops, bytes_accessed=moved, transcendentals=0),
    )(*args, *late)


def body(prior, data, taps, offsets, coverage):
    nview, nspace = lax.axis_size("view"), lax.axis_size("space")
    g, j = lax.axis_index("view"), lax.axis_index("space")
    zh, yh = g >> 1, (g ^ (g >> 1)) & 1
    place_yz = jnp.stack([yh, zh, j]).astype(jnp.int32)
    local, width, ny, nz = data.shape
    ntaps = taps.shape[-1]
    rad = ntaps // 2
    hy, hz = ny // 2, nz // 2
    wy = hy + rad
    group = hz // rad
    half, rims = wy // 2, wy // 2 // group
    rows = half + rims

    flat = jnp.concatenate(
        [
            taps.reshape(local, -1),
            offsets.astype(jnp.float32)[:, None],
            coverage.astype(jnp.float32),
        ],
        axis=1,
    )
    used = flat.shape[1]
    flat = jnp.pad(flat, ((0, 0), (0, -used % LANES)))
    shared = [flat] + [swap(flat, "view", r) for r in range(1, nview)]
    shared = jnp.concatenate(shared, axis=0)

    def quadrant(owner):
        oz, oy = owner >> 1, (owner ^ (owner >> 1)) & 1
        return lax.dynamic_slice(data, (0, 0, oy * hy, oz * hz), (local, width, hy, hz))

    pieces = [quadrant(g)] + [swap(quadrant(g ^ r), "view", r) for r in range(1, nview)]

    nviews = nview * local
    nvi = nviews * width
    kern = shared[:, : 3 * ntaps].reshape(nviews, 3, ntaps)
    kern = kern / jnp.sum(kern, axis=-1, keepdims=True)
    turn = shared[:, 3 * ntaps].astype(jnp.int32)
    cover = shared[:, 3 * ntaps + 1 : used]
    count = jnp.broadcast_to(jnp.sum(cover, axis=0)[:, None], (width, hz))
    note = jnp.pad(cover.T, ((0, 0), (0, hz - nviews)))[None]

    window = lax.dynamic_slice_in_dim(prior, rad * yh, wy, axis=1).transpose(1, 0, 2)
    main = lax.dynamic_slice_in_dim(window, hz * zh, hz, axis=2)
    rim = lax.dynamic_slice_in_dim(window, jnp.where(zh == 0, hz, hz - rad), rad, axis=2)
    rim = rim.reshape(2 * rims, group, width, rad).transpose(0, 2, 1, 3).reshape(2 * rims, width, hz)
    parts = [main[:half], rim[:rims], main[half:], rim[rims:]]
    estimate = [jnp.concatenate(parts[:2], axis=0), jnp.concatenate(parts[2:], axis=0)]
    wide = gather(estimate)
    notes = gather([note])

    nx = nspace * width
    wx, bxt, kz, kzt = pl.pallas_call(
        functools.partial(bands_kernel, rad),
        out_shape=[
            jax.ShapeDtypeStruct((nvi, 3 * nx), BF16),
            jax.ShapeDtypeStruct((nx, nvi), F32),
            jax.ShapeDtypeStruct((nviews, 4 * hz, hz), BF16),
            jax.ShapeDtypeStruct((nviews, 3 * hz, 2 * hz), BF16),
        ],
        in_specs=[SMEM] * 3,
        out_specs=[VMEM] * 4,
        compiler_params=PARAMS,
        cost_estimate=pl.CostEstimate(flops=nviews * hz * hz * 32, bytes_accessed=nviews * hz * hz * 16, transcendentals=0),
    )(place_yz, (j - turn) % nspace, kern.reshape(nviews, -1))
    ky = kern[:, 1]

    plane = width * hz
    mxu = 2 * 3 * nvi * plane * 2 * rows * (nspace // 2)

    def ahead(wide, late, cost):
        return call(
            functools.partial(ahead_kernel, rad),
            [(hy, nvi, hz)],
            [(wy, nvi, hz), pltpu.VMEM((wy, nvi, hz), BF16), (wy + rad, width, hz), (wy + rad, width, hz)],
            2,
            cost,
            place_yz, ky, wx, kz, *wide,
            late=late,
        )[0]

    def back(blurred):
        return call(
            functools.partial(back_kernel, rad, nview),
            [(nspace // 2, 2 * rows, width, hz)] * 2,
            [(hy, nvi, hz), (hy + 2 * rad, width, hz), (hy + 2 * rad, width, hz), (wy, nvi, hz), (2 * rims, nvi, hz), pltpu.VMEM((nx, 3 * nvi), BF16)],
            2,
            (mxu, 4 * plane * (nspace * 2 * rows + 2 * hy * nviews)),
            place_yz, ky, bxt, *notes, kzt, blurred, *pieces,
        )

    over = hy // group
    for step in range(ITERS):
        if step:
            wide = gather(estimate)
        blurred = ahead(wide, () if step else tuple(pieces[1:3]), (mxu if step else 0, plane))
        a, b = scatter_sum(*back(blurred))
        last = step == ITERS - 1
        if last:
            sizes, scratch = (rad, over, rad // group), []
            results = [(width, hy, hz)]
        else:
            sizes, scratch = (hy + over, 4 * rims, 2 * over), [(2 * rims, width, hz)]
            results = [(rows, width, hz)] * 2
        to_y, to_z, to_c = call(
            functools.partial(last_pack_kernel if last else pack_kernel, rad),
            [(size, width, hz) for size in sizes],
            scratch,
            1,
            (plane, 4 * plane * 4 * rows),
            place_yz, a, b,
        )
        estimate = call(
            functools.partial(last_update_kernel if last else update_kernel, rad),
            results,
            [],
            1,
            (plane, 4 * plane * 8 * rows),
            place_yz, a, b, swap(to_y, "view", 1), swap(to_z, "view", 3), swap(to_c, "view", 2), *estimate, count,
        )

    own = estimate[0]
    parts = [own] + [swap(own, "view", r) for r in range(1, nview)]
    return call(
        assemble_kernel,
        [(width, ny, nz)],
        [],
        1,
        (plane, 16 * plane * ny),
        g.astype(jnp.int32)[None], *parts,
    )[0]


def solution(mesh):
    return jax.shard_map(
        body,
        mesh=mesh,
        in_specs=(
            P("space", None, None),
            P("view", "space", None, None),
            P("view", None, None),
            P("view"),
            P("view", "space"),
        ),
        out_specs=P("space", None, None),
        check_vma=False,
    )
```

```python
import functools

import jax
import jax.numpy as jnp
from jax import lax
from jax.experimental import pallas as pl
from jax.experimental.pallas import tpu as pltpu
from jax.sharding import PartitionSpec as P

ITERS = 2
LANES = 128
BLOCK = 8
F32, BF16 = jnp.float32, jnp.bfloat16
PARAMS = pltpu.CompilerParams(vmem_limit_bytes=58 * 1024 * 1024)


def swap(value, axis, mask):
    count = lax.axis_size(axis)
    return lax.ppermute(value, axis, [(i, i ^ mask) for i in range(count)])


def orders(bits):
    shift = (bits - 1) // 2
    upper = list(range(1, bits))
    return upper, upper[shift:] + upper[:shift]


def scatter_sum(kept, sent):
    bits = lax.axis_size("space").bit_length() - 1
    out = []
    for part, other, order in zip(kept, sent, orders(bits)):
        part = part + swap(other, "space", 1)
        left = list(range(1, bits))
        for bit in order:
            low = 1 << left.index(bit)
            split = part.reshape((part.shape[0] // (2 * low), 2, low) + part.shape[1:])
            part = split[:, 0] + swap(split[:, 1], "space", 1 << bit)
            part = part.reshape((-1,) + part.shape[2:])
            left.remove(bit)
        out.append(part[0])
    return out


def gather(parts):
    bits = lax.axis_size("space").bit_length() - 1
    out = []
    for part, order in zip(parts, orders(bits)):
        part = part[None]
        have = []
        for bit in reversed(order):
            low = 1 << sum(other < bit for other in have)
            part = part.reshape((part.shape[0] // low, 1, low) + part.shape[1:])
            part = jnp.concatenate([part, swap(part, "space", 1 << bit)], axis=1)
            part = part.reshape((-1,) + part.shape[3:])
            have.append(bit)
        out += [part, swap(part, "space", 1)]
    return out


def split(value):
    high = value.astype(BF16)
    return high, (value - high.astype(F32)).astype(BF16)


def stack3(value):
    high, low = split(value)
    return jnp.concatenate([high, low, high], axis=0)


def mul(a, b):
    return jnp.dot(a, b, preferred_element_type=F32)


def lane_of(shape):
    return lax.broadcasted_iota(jnp.int32, shape, len(shape) - 1)


def bands_kernel(rad, place, slab, kern, wx, bxt, kz, kzt):
    zh, j = place[1], place[2]
    nx, nvi = bxt.shape
    nviews, _, hz = kz.shape
    width = nvi // nviews
    taps = 2 * rad

    def taken(v, axis, index):
        total = jnp.zeros(index.shape, F32)
        for t in range(taps):
            total = jnp.where(index == t, kern[v, axis * taps + t], total)
        return total

    shape = (width, nx)
    lane, row = lane_of(shape), lax.broadcasted_iota(jnp.int32, shape, 0)
    block = lane // width
    blocks = nx // width // 2
    block = jnp.bitwise_xor(2 * (block % blocks) + block // blocks, jnp.full(shape, j, jnp.int32))
    cell = block * width + lane % width - row + rad
    for v in range(nviews):
        value = taken(v, 0, cell - slab[v] * width)
        high, low = split(value)
        at = pl.ds(v * width, width)
        wx[at, :nx] = high
        wx[at, nx : 2 * nx] = high
        wx[at, 2 * nx :] = low
        bxt[:, v * width : (v + 1) * width] = value.T
    shape = (hz, hz)
    middle = lax.broadcasted_iota(jnp.int32, shape, 0) - lane_of(shape) + rad
    shape = (rad, hz)
    outer = lax.broadcasted_iota(jnp.int32, shape, 0) - lane_of(shape) + (hz + rad) * (1 - zh)

    def one(v, carry):
        main, rim = taken(v, 2, middle), taken(v, 2, outer)
        high, low = split(main)
        rim_high, rim_low = split(rim)
        rest = jnp.zeros((hz - 3 * rad, hz), BF16)
        kz[v] = jnp.concatenate([high, high, low, rim_high, rim_high, rim_low, rest], axis=0)
        rim = jnp.concatenate([rim, jnp.zeros((hz - rad, hz), F32)], axis=0)
        high, low = split(jnp.concatenate([main.T, rim.T], axis=1))
        kzt[v] = jnp.concatenate([high, high, low], axis=0)
        return carry

    lax.fori_loop(0, nviews, one, 0)


def ahead_kernel(rad, place, ky, wx, kz, a0, a1, b0, b1, *refs):
    blurred, u, uh, za, zb = refs[-5:]
    yh = place[0]
    wy, nvi, hz = u.shape
    hy = blurred.shape[0]
    width = a0.shape[2]
    nviews = nvi // width
    half, group = wy // 2, hz // rad
    part = lane_of((nvi, hz)) // rad
    for h, pair in enumerate(((a0, a1), (b0, b1))):

        def row(y):
            return jnp.concatenate([ref[k, y] for ref in pair for k in range(ref.shape[0])], axis=0)

        for k in range(half // group):
            out = mul(wx[...], stack3(row(half + k)))
            high = out.astype(BF16).astype(F32)
            low = out - high
            for m in range(group):
                first, second, third = (
                    pltpu.roll(value, (rad * (at - m)) % hz, 1) if at != m else value
                    for at, value in enumerate((high, low, high))
                )
                value = jnp.where(part == 0, first, jnp.where(part == 1, second, jnp.where(part == 2, third, 0.0)))
                uh[h * half + k * group + m] = value.astype(BF16)

        for y in range(0, half, 2):
            out = mul(wx[...], stack3(jnp.concatenate([row(y), row(y + 1)], axis=1)))
            u[h * half + y] = out[:, :hz]
            u[h * half + y + 1] = out[:, hz:]

    lead = rad * (1 - yh)
    for z in (za, zb):
        z[pl.ds(wy * yh, rad)] = jnp.zeros((rad, width, hz), F32)

    def along_z(v, z):
        at = pl.ds(pl.multiple_of(v * width, width), width)
        high, low = split(u[:, at, :].reshape(wy * width, hz))
        value = jnp.concatenate([high, low, high, uh[:, at, :].reshape(wy * width, hz)], axis=1)
        z[pl.ds(lead, wy)] = mul(value, kz[v]).reshape(wy, width, hz)

    def along_y(v, z):
        tap = [ky[v, t] for t in range(2 * rad)]
        for s in range(0, width, 8):
            for first in range(0, hy, BLOCK):
                total = [None] * BLOCK
                for y in range(first, first + BLOCK + 2 * rad - 1):
                    value = z[y, s : s + 8, :]
                    for k in range(BLOCK):
                        t = y - first - k
                        if 0 <= t < 2 * rad:
                            term = tap[t] * value
                            total[k] = term if total[k] is None else total[k] + term
                for k in range(BLOCK):
                    blurred[first + k, pl.ds(pl.multiple_of(v * width + s, 8), 8), :] = total[k]

    along_z(0, za)

    def views(p, carry):
        along_z(2 * p + 1, zb)
        along_y(2 * p, za)
        along_z(jnp.minimum(2 * p + 2, nviews - 1), za)
        along_y(2 * p + 1, zb)
        return carry

    lax.fori_loop(0, nviews // 2, views, 0)


def back_kernel(rad, npieces, place, ky, bxt, note0, note1, kz, blurred, *refs):
    pieces, outs, (r, ya, yb, gm, gh, wxt) = refs[:npieces], refs[npieces : npieces + 4], refs[npieces + 4 :]
    yh = place[0]
    hy, nvi, hz = blurred.shape
    wy = gm.shape[0]
    local, width = pieces[0].shape[:2]
    nviews = nvi // width
    half, group = wy // 2, hz // rad
    rims = half // group
    cover = jnp.concatenate([ref[k, 0] for ref in (note0, note1) for k in range(ref.shape[0])], axis=0)
    shape = (hz, nvi)
    spread = jnp.where(lane_of(shape) // width == lax.broadcasted_iota(jnp.int32, shape, 0), 1.0, 0.0)
    high, low = split(bxt[...] * mul(cover.astype(BF16), spread.astype(BF16)))
    wxt[...] = jnp.concatenate([high, high, low], axis=1)
    for p, piece in enumerate(pieces):
        for k in range(local):
            first = (p * local + k) * width
            for y in range(hy):
                r[y, first : first + width, :] = piece[k, :, y, :] / blurred[y, first : first + width, :]

    lead = rad * (1 - yh)

    def along_y(v, out):
        tap = [ky[v, t] for t in range(2 * rad)]
        for s in range(0, width, 8):
            at = pl.ds(pl.multiple_of(v * width + s, 8), 8)
            for first in range(0, hy + 2 * rad, BLOCK):
                total = [None] * BLOCK
                for y in range(max(0, first - 2 * rad + 1), min(hy, first + BLOCK)):
                    value = r[y, at, :]
                    for k in range(BLOCK):
                        t = first + k - y
                        if 0 <= t < 2 * rad:
                            term = tap[t] * value
                            total[k] = term if total[k] is None else total[k] + term
                for k in range(BLOCK):
                    out[first + k, s : s + 8, :] = jnp.zeros((8, hz), F32) if total[k] is None else total[k]

    def along_z(v, y):
        at = pl.ds(pl.multiple_of(v * width, width), width)
        high, low = split(y[pl.ds(lead, wy)].reshape(wy * width, hz))
        out = mul(jnp.concatenate([high, low, high], axis=1), kz[v]).reshape(wy, width, 2 * hz)
        gm[:, at, :] = out[..., :hz]
        for o in range(2 * rims):
            total = out[o * group, :, hz:]
            for m in range(1, group):
                total = total + pltpu.roll(out[o * group + m, :, hz:], rad * m, 1)
            gh[o, at, :] = total

    along_y(0, ya)

    def views(p, carry):
        along_y(2 * p + 1, yb)
        along_z(2 * p, ya)
        along_y(jnp.minimum(2 * p + 2, nviews - 1), ya)
        along_z(2 * p + 1, yb)
        return carry

    lax.fori_loop(0, nviews // 2, views, 0)

    def store(out, row):
        h, row = divmod(row, half + rims)
        for c in range(2):
            ref = outs[2 * c + h]
            for k in range(ref.shape[0]):
                first = (c * ref.shape[0] + k) * width
                ref[k, row] = out[first : first + width]

    for c in range(2):
        for k in range(rims):
            store(mul(wxt[...], stack3(gh[c * rims + k])), c * (half + rims) + half + k)

        for y in range(c * half, (c + 1) * half, 2):
            out = mul(wxt[...], stack3(jnp.concatenate([gm[y], gm[y + 1]], axis=1)))
            store(out[:, :hz], c * rims + y)
            store(out[:, hz:], c * rims + y + 1)


def row_of(a, b, y, half):
    return a[y] if y < half else b[y - half]


def pack_kernel(rad, place, a, b, to_y, to_z, to_c, edge):
    yh, zh = place[0], place[1]
    rows, width, hz = a.shape
    group = hz // rad
    half = rows * group // (group + 1)
    rims, wy = half // group, 2 * half
    begin = (hz - rad) * (1 - zh)
    lane = lane_of((width, hz)) // rad
    for o in range(2 * rims):
        total = None
        for m in range(group):
            value = pltpu.roll(row_of(a, b, o * group + m, half), (rad * m - begin + hz) % hz, 1)
            total = value if m == 0 else jnp.where(lane == m, value, total)
        edge[o] = total
        to_z[2 * rims + o] = total
        to_z[o] = (a if o < rims else b)[half + o % rims]
    hy = wy - rad
    over = hy // group
    for y in range(wy):
        @pl.when(jnp.logical_and(y >= rad * (1 - yh), y < rad * (1 - yh) + hy))
        def _():
            to_y[y - rad * (1 - yh)] = row_of(a, b, y, half)
    skip = (rad // group) * (1 - yh)
    for k in range(over):
        to_y[hy + k] = to_z[skip + k]
        to_c[k] = to_z[skip + k]
        to_c[over + k] = edge[skip + k]


def update_kernel(rad, place, a, b, fy, fz, fc, old_a, old_b, count, new_a, new_b):
    yh, zh = place[0], place[1]
    rows, width, hz = a.shape
    group = hz // rad
    half = rows * group // (group + 1)
    rims, wy = half // group, 2 * half
    hy = wy - rad
    over = hy // group
    start, skip = rad * (1 - yh), (rad // group) * (1 - yh)
    begin = (hz - rad) * (1 - zh)
    zero = jnp.zeros((width, hz), F32)
    inside = (lane_of((width, hz)) >= begin) & (lane_of((width, hz)) < begin + rad)
    total = count[...]

    def part(ref, first, at, limit):
        ok = jnp.logical_and(at >= 0, at < limit)
        return jnp.where(ok, ref[first + jnp.clip(at, 0, limit - 1)], zero)

    for o in range(2 * rims):
        h, k = o // rims, o % rims
        old, new, row = (old_a, old_b)[h], (new_a, new_b)[h], half + k
        rim = (a, b)[h][half + k] + fz[2 * rims + o]
        rim = rim + part(fy, hy, o - skip, over) + part(fc, over, o - skip, over)
        new[row] = old[row] * rim / total
        edge = fz[o] + part(fc, 0, o - skip, over)
        for m in range(group):
            y = o * group + m
            moved = jnp.where(inside, pltpu.roll(edge, (begin - rad * m + hz) % hz, 1), 0.0)
            value = row_of(a, b, y, half) + part(fy, 0, y - start, hy) + moved
            row = y - h * half
            new[row] = old[row] * value / total


def last_pack_kernel(rad, place, a, b, to_y, to_z, to_c):
    rows, _, hz = a.shape
    group = hz // rad
    half = rows * group // (group + 1)
    rims, own = half // group, 2 * half - rad
    for side in range(2):

        @pl.when(place[0] == side)
        def _():
            outer = own * (1 - side)
            for k in range(rad):
                to_y[k] = row_of(a, b, outer + k, half)
            for ref, first in ((to_z, rad * side // group), (to_c, outer // group)):
                for k in range(ref.shape[0]):
                    o = first + k
                    ref[k] = (a if o < rims else b)[half + o % rims]


def last_update_kernel(rad, place, a, b, fy, fz, fc, old_a, old_b, count, new):
    rows, width, hz = a.shape
    group = hz // rad
    half = rows * group // (group + 1)
    own = new.shape[1]
    begin = (hz - rad) * (1 - place[1])
    inside = (lane_of((width, hz)) >= begin) & (lane_of((width, hz)) < begin + rad)
    total = count[...]
    for side in range(2):

        @pl.when(place[0] == side)
        def _():
            first = (own - rad) * (1 - side)
            for k in range(own):
                y = rad * side + k
                value, edge = row_of(a, b, y, half), fz[k // group]
                if first <= k < first + rad:
                    value = value + fy[k - first]
                    edge = edge + fc[(k - first) // group]
                moved = pltpu.roll(edge, (begin - rad * (k % group) + hz) % hz, 1)
                value = value + jnp.where(inside, moved, 0.0)
                new[:, k, :] = row_of(old_a, old_b, y, half) * value / total


def assemble_kernel(where, *refs):
    pieces, out = refs[:-1], refs[-1]
    _, hy, hz = pieces[0].shape
    for r, piece in enumerate(pieces):
        for owner in range(len(pieces)):
            oz, oy = owner >> 1, (owner ^ (owner >> 1)) & 1

            @pl.when(where[0] == owner ^ r)
            def _():
                out[:, oy * hy : (oy + 1) * hy, oz * hz : (oz + 1) * hz] = piece[...]


VMEM = pl.BlockSpec(memory_space=pltpu.VMEM)
ANY = pl.BlockSpec(memory_space=pl.ANY)
SMEM = pl.BlockSpec(memory_space=pltpu.SMEM)


def call(kernel, shapes, scratch, smem, cost, *args, late=()):
    flops, moved = cost
    return pl.pallas_call(
        kernel,
        out_shape=[jax.ShapeDtypeStruct(shape, F32) for shape in shapes],
        in_specs=[SMEM] * smem + [VMEM] * (len(args) - smem) + [ANY] * len(late),
        out_specs=[VMEM] * len(shapes),
        scratch_shapes=[pltpu.VMEM(s, F32) if isinstance(s, tuple) else s for s in scratch],
        compiler_params=PARAMS,
        cost_estimate=pl.CostEstimate(flops=flops, bytes_accessed=moved, transcendentals=0),
    )(*args, *late)


def body(prior, data, taps, offsets, coverage):
    nview, nspace = lax.axis_size("view"), lax.axis_size("space")
    g, j = lax.axis_index("view"), lax.axis_index("space")
    zh, yh = g >> 1, (g ^ (g >> 1)) & 1
    place_yz = jnp.stack([yh, zh, j]).astype(jnp.int32)
    local, width, ny, nz = data.shape
    ntaps = taps.shape[-1]
    rad = ntaps // 2
    hy, hz = ny // 2, nz // 2
    wy = hy + rad
    group = hz // rad
    half, rims = wy // 2, wy // 2 // group
    rows = half + rims

    flat = jnp.concatenate(
        [
            taps.reshape(local, -1),
            offsets.astype(jnp.float32)[:, None],
            coverage.astype(jnp.float32),
        ],
        axis=1,
    )
    used = flat.shape[1]
    flat = jnp.pad(flat, ((0, 0), (0, -used % LANES)))
    shared = [flat] + [swap(flat, "view", r) for r in range(1, nview)]
    shared = jnp.concatenate(shared, axis=0)

    def quadrant(owner):
        oz, oy = owner >> 1, (owner ^ (owner >> 1)) & 1
        return lax.dynamic_slice(data, (0, 0, oy * hy, oz * hz), (local, width, hy, hz))

    pieces = [quadrant(g)] + [swap(quadrant(g ^ r), "view", r) for r in range(1, nview)]

    nviews = nview * local
    nvi = nviews * width
    kern = shared[:, : 3 * ntaps].reshape(nviews, 3, ntaps)
    kern = kern / jnp.sum(kern, axis=-1, keepdims=True)
    turn = shared[:, 3 * ntaps].astype(jnp.int32)
    cover = shared[:, 3 * ntaps + 1 : used]
    count = jnp.broadcast_to(jnp.sum(cover, axis=0)[:, None], (width, hz))
    note = jnp.pad(cover.T, ((0, 0), (0, hz - nviews)))[None]

    window = lax.dynamic_slice_in_dim(prior, rad * yh, wy, axis=1).transpose(1, 0, 2)
    main = lax.dynamic_slice_in_dim(window, hz * zh, hz, axis=2)
    rim = lax.dynamic_slice_in_dim(window, jnp.where(zh == 0, hz, hz - rad), rad, axis=2)
    rim = rim.reshape(2 * rims, group, width, rad).transpose(0, 2, 1, 3).reshape(2 * rims, width, hz)
    parts = [main[:half], rim[:rims], main[half:], rim[rims:]]
    estimate = [jnp.concatenate(parts[:2], axis=0), jnp.concatenate(parts[2:], axis=0)]
    wide = gather(estimate)
    notes = gather([note])

    nx = nspace * width
    wx, bxt, kz, kzt = pl.pallas_call(
        functools.partial(bands_kernel, rad),
        out_shape=[
            jax.ShapeDtypeStruct((nvi, 3 * nx), BF16),
            jax.ShapeDtypeStruct((nx, nvi), F32),
            jax.ShapeDtypeStruct((nviews, 4 * hz, hz), BF16),
            jax.ShapeDtypeStruct((nviews, 3 * hz, 2 * hz), BF16),
        ],
        in_specs=[SMEM] * 3,
        out_specs=[VMEM] * 4,
        compiler_params=PARAMS,
        cost_estimate=pl.CostEstimate(flops=nviews * hz * hz * 32, bytes_accessed=nviews * hz * hz * 16, transcendentals=0),
    )(place_yz, (j - turn) % nspace, kern.reshape(nviews, -1))
    ky = kern[:, 1]

    plane = width * hz
    mxu = 2 * 3 * nvi * plane * 2 * rows * (nspace // 2)

    def ahead(wide, late, cost):
        return call(
            functools.partial(ahead_kernel, rad),
            [(hy, nvi, hz)],
            [(wy, nvi, hz), pltpu.VMEM((wy, nvi, hz), BF16), (wy + rad, width, hz), (wy + rad, width, hz)],
            2,
            cost,
            place_yz, ky, wx, kz, *wide,
            late=late,
        )[0]

    def back(blurred):
        return call(
            functools.partial(back_kernel, rad, nview),
            [(nspace // 2, rows, width, hz)] * 4,
            [(hy, nvi, hz), (hy + 2 * rad, width, hz), (hy + 2 * rad, width, hz), (wy, nvi, hz), (2 * rims, nvi, hz), pltpu.VMEM((nx, 3 * nvi), BF16)],
            2,
            (mxu, 4 * plane * (nspace * 2 * rows + 2 * hy * nviews)),
            place_yz, ky, bxt, *notes, kzt, blurred, *pieces,
        )

    over = hy // group
    for step in range(ITERS):
        if step:
            wide = gather(estimate)
        blurred = ahead(wide, () if step else tuple(pieces[1:3]), (mxu if step else 0, plane))
        sums = back(blurred)
        a, b = scatter_sum(sums[:2], sums[2:])
        last = step == ITERS - 1
        if last:
            sizes, scratch = (rad, over, rad // group), []
            results = [(width, hy, hz)]
        else:
            sizes, scratch = (hy + over, 4 * rims, 2 * over), [(2 * rims, width, hz)]
            results = [(rows, width, hz)] * 2
        to_y, to_z, to_c = call(
            functools.partial(last_pack_kernel if last else pack_kernel, rad),
            [(size, width, hz) for size in sizes],
            scratch,
            1,
            (plane, 4 * plane * 4 * rows),
            place_yz, a, b,
        )
        estimate = call(
            functools.partial(last_update_kernel if last else update_kernel, rad),
            results,
            [],
            1,
            (plane, 4 * plane * 8 * rows),
            place_yz, a, b, swap(to_y, "view", 1), swap(to_z, "view", 3), swap(to_c, "view", 2), *estimate, count,
        )

    own = estimate[0]
    parts = [own] + [swap(own, "view", r) for r in range(1, nview)]
    return call(
        assemble_kernel,
        [(width, ny, nz)],
        [],
        1,
        (plane, 16 * plane * ny),
        g.astype(jnp.int32)[None], *parts,
    )[0]


def solution(mesh):
    return jax.shard_map(
        body,
        mesh=mesh,
        in_specs=(
            P("space", None, None),
            P("view", "space", None, None),
            P("view", None, None),
            P("view"),
            P("view", "space"),
        ),
        out_specs=P("space", None, None),
        check_vma=False,
    )
```

```python
import functools

import jax
import jax.numpy as jnp
from jax import lax
from jax.experimental import pallas as pl
from jax.experimental.pallas import tpu as pltpu
from jax.sharding import PartitionSpec as P

ITERS = 2
LANES = 128
BLOCK = 16
F32, BF16 = jnp.float32, jnp.bfloat16
PARAMS = pltpu.CompilerParams(vmem_limit_bytes=58 * 1024 * 1024)


def swap(value, axis, mask):
    count = lax.axis_size(axis)
    return lax.ppermute(value, axis, [(i, i ^ mask) for i in range(count)])


def orders(bits):
    shift = (bits - 1) // 2
    upper = list(range(1, bits))
    return upper, upper[shift:] + upper[:shift]


def scatter_sum(kept, sent):
    bits = lax.axis_size("space").bit_length() - 1
    out = []
    for part, other, order in zip(kept, sent, orders(bits)):
        part = part + swap(other, "space", 1)
        left = list(range(1, bits))
        for bit in order:
            low = 1 << left.index(bit)
            split = part.reshape((part.shape[0] // (2 * low), 2, low) + part.shape[1:])
            part = split[:, 0] + swap(split[:, 1], "space", 1 << bit)
            part = part.reshape((-1,) + part.shape[2:])
            left.remove(bit)
        out.append(part[0])
    return out


def gather(parts):
    bits = lax.axis_size("space").bit_length() - 1
    out = []
    for part, order in zip(parts, orders(bits)):
        part = part[None]
        have = []
        for bit in reversed(order):
            low = 1 << sum(other < bit for other in have)
            part = part.reshape((part.shape[0] // low, 1, low) + part.shape[1:])
            part = jnp.concatenate([part, swap(part, "space", 1 << bit)], axis=1)
            part = part.reshape((-1,) + part.shape[3:])
            have.append(bit)
        out += [part, swap(part, "space", 1)]
    return out


def split(value):
    high = value.astype(BF16)
    return high, (value - high.astype(F32)).astype(BF16)


def stack3(value):
    high, low = split(value)
    return jnp.concatenate([high, low, high], axis=0)


def mul(a, b):
    return jnp.dot(a, b, preferred_element_type=F32)


def lane_of(shape):
    return lax.broadcasted_iota(jnp.int32, shape, len(shape) - 1)


def bands_kernel(rad, place, slab, kern, wx, bxt, kz, kzt):
    zh, j = place[1], place[2]
    nx, nvi = bxt.shape
    nviews, _, hz = kz.shape
    width = nvi // nviews
    taps = 2 * rad

    def taken(v, axis, index):
        total = jnp.zeros(index.shape, F32)
        for t in range(taps):
            total = jnp.where(index == t, kern[v, axis * taps + t], total)
        return total

    shape = (width, nx)
    lane, row = lane_of(shape), lax.broadcasted_iota(jnp.int32, shape, 0)
    block = lane // width
    blocks = nx // width // 2
    block = jnp.bitwise_xor(2 * (block % blocks) + block // blocks, jnp.full(shape, j, jnp.int32))
    cell = block * width + lane % width - row + rad
    for v in range(nviews):
        value = taken(v, 0, cell - slab[v] * width)
        high, low = split(value)
        at = pl.ds(v * width, width)
        wx[at, :nx] = high
        wx[at, nx : 2 * nx] = high
        wx[at, 2 * nx :] = low
        bxt[:, v * width : (v + 1) * width] = value.T
    shape = (hz, hz)
    middle = lax.broadcasted_iota(jnp.int32, shape, 0) - lane_of(shape) + rad
    shape = (rad, hz)
    outer = lax.broadcasted_iota(jnp.int32, shape, 0) - lane_of(shape) + (hz + rad) * (1 - zh)

    def one(v, carry):
        main, rim = taken(v, 2, middle), taken(v, 2, outer)
        high, low = split(main)
        rim_high, rim_low = split(rim)
        rest = jnp.zeros((hz - 3 * rad, hz), BF16)
        kz[v] = jnp.concatenate([high, high, low, rim_high, rim_high, rim_low, rest], axis=0)
        rim = jnp.concatenate([rim, jnp.zeros((hz - rad, hz), F32)], axis=0)
        high, low = split(jnp.concatenate([main.T, rim.T], axis=1))
        kzt[v] = jnp.concatenate([high, high, low], axis=0)
        return carry

    lax.fori_loop(0, nviews, one, 0)


def ahead_kernel(rad, place, ky, wx, kz, a0, a1, b0, b1, *refs):
    blurred, u, uh, za, zb = refs[-5:]
    yh = place[0]
    wy, nvi, hz = u.shape
    hy = blurred.shape[0]
    width = a0.shape[2]
    nviews = nvi // width
    half, group = wy // 2, hz // rad
    part = lane_of((nvi, hz)) // rad
    for h, pair in enumerate(((a0, a1), (b0, b1))):

        def row(y):
            return jnp.concatenate([ref[k, y] for ref in pair for k in range(ref.shape[0])], axis=0)

        for k in range(half // group):
            out = mul(wx[...], stack3(row(half + k)))
            high = out.astype(BF16).astype(F32)
            low = out - high
            for m in range(group):
                first, second, third = (
                    pltpu.roll(value, (rad * (at - m)) % hz, 1) if at != m else value
                    for at, value in enumerate((high, low, high))
                )
                value = jnp.where(part == 0, first, jnp.where(part == 1, second, jnp.where(part == 2, third, 0.0)))
                uh[h * half + k * group + m] = value.astype(BF16)

        for y in range(0, half, 2):
            out = mul(wx[...], stack3(jnp.concatenate([row(y), row(y + 1)], axis=1)))
            u[h * half + y] = out[:, :hz]
            u[h * half + y + 1] = out[:, hz:]

    lead = rad * (1 - yh)
    for z in (za, zb):
        z[pl.ds(wy * yh, rad)] = jnp.zeros((rad, width, hz), F32)

    def along_z(v, z):
        at = pl.ds(pl.multiple_of(v * width, width), width)
        high, low = split(u[:, at, :].reshape(wy * width, hz))
        value = jnp.concatenate([high, low, high, uh[:, at, :].reshape(wy * width, hz)], axis=1)
        z[pl.ds(lead, wy)] = mul(value, kz[v]).reshape(wy, width, hz)

    def along_y(v, z):
        tap = [ky[v, t] for t in range(2 * rad)]
        for s in range(0, width, 8):
            for first in range(0, hy, BLOCK):
                total = [None] * BLOCK
                for y in range(first, first + BLOCK + 2 * rad - 1):
                    value = z[y, s : s + 8, :]
                    for k in range(BLOCK):
                        t = y - first - k
                        if 0 <= t < 2 * rad:
                            term = tap[t] * value
                            total[k] = term if total[k] is None else total[k] + term
                for k in range(BLOCK):
                    blurred[first + k, pl.ds(pl.multiple_of(v * width + s, 8), 8), :] = total[k]

    along_z(0, za)

    def views(p, carry):
        along_z(2 * p + 1, zb)
        along_y(2 * p, za)
        along_z(jnp.minimum(2 * p + 2, nviews - 1), za)
        along_y(2 * p + 1, zb)
        return carry

    lax.fori_loop(0, nviews // 2, views, 0)


def back_kernel(rad, npieces, place, ky, bxt, note0, note1, kz, blurred, *refs):
    pieces, outs, (r, ya, yb, gm, gh, wxt) = refs[:npieces], refs[npieces : npieces + 4], refs[npieces + 4 :]
    yh = place[0]
    hy, nvi, hz = blurred.shape
    wy = gm.shape[0]
    local, width = pieces[0].shape[:2]
    nviews = nvi // width
    half, group = wy // 2, hz // rad
    rims = half // group
    cover = jnp.concatenate([ref[k, 0] for ref in (note0, note1) for k in range(ref.shape[0])], axis=0)
    shape = (hz, nvi)
    spread = jnp.where(lane_of(shape) // width == lax.broadcasted_iota(jnp.int32, shape, 0), 1.0, 0.0)
    high, low = split(bxt[...] * mul(cover.astype(BF16), spread.astype(BF16)))
    wxt[...] = jnp.concatenate([high, high, low], axis=1)
    for p, piece in enumerate(pieces):
        for k in range(local):
            first = (p * local + k) * width
            for y in range(hy):
                r[y, first : first + width, :] = piece[k, :, y, :] / blurred[y, first : first + width, :]

    lead = rad * (1 - yh)

    def along_y(v, out):
        tap = [ky[v, t] for t in range(2 * rad)]
        for s in range(0, width, 8):
            at = pl.ds(pl.multiple_of(v * width + s, 8), 8)
            for first in range(0, hy + 2 * rad, BLOCK):
                total = [None] * BLOCK
                for y in range(max(0, first - 2 * rad + 1), min(hy, first + BLOCK)):
                    value = r[y, at, :]
                    for k in range(BLOCK):
                        t = first + k - y
                        if 0 <= t < 2 * rad:
                            term = tap[t] * value
                            total[k] = term if total[k] is None else total[k] + term
                for k in range(BLOCK):
                    out[first + k, s : s + 8, :] = jnp.zeros((8, hz), F32) if total[k] is None else total[k]

    def along_z(v, y):
        at = pl.ds(pl.multiple_of(v * width, width), width)
        high, low = split(y[pl.ds(lead, wy)].reshape(wy * width, hz))
        out = mul(jnp.concatenate([high, low, high], axis=1), kz[v]).reshape(wy, width, 2 * hz)
        gm[:, at, :] = out[..., :hz]
        for o in range(2 * rims):
            total = out[o * group, :, hz:]
            for m in range(1, group):
                total = total + pltpu.roll(out[o * group + m, :, hz:], rad * m, 1)
            gh[o, at, :] = total

    along_y(0, ya)

    def views(p, carry):
        along_y(2 * p + 1, yb)
        along_z(2 * p, ya)
        along_y(jnp.minimum(2 * p + 2, nviews - 1), ya)
        along_z(2 * p + 1, yb)
        return carry

    lax.fori_loop(0, nviews // 2, views, 0)

    def store(out, row):
        h, row = divmod(row, half + rims)
        for c in range(2):
            ref = outs[2 * c + h]
            for k in range(ref.shape[0]):
                first = (c * ref.shape[0] + k) * width
                ref[k, row] = out[first : first + width]

    for c in range(2):
        for k in range(rims):
            store(mul(wxt[...], stack3(gh[c * rims + k])), c * (half + rims) + half + k)

        for y in range(c * half, (c + 1) * half, 2):
            out = mul(wxt[...], stack3(jnp.concatenate([gm[y], gm[y + 1]], axis=1)))
            store(out[:, :hz], c * rims + y)
            store(out[:, hz:], c * rims + y + 1)


def row_of(a, b, y, half):
    return a[y] if y < half else b[y - half]


def pack_kernel(rad, place, a, b, to_y, to_z, to_c, edge):
    yh, zh = place[0], place[1]
    rows, width, hz = a.shape
    group = hz // rad
    half = rows * group // (group + 1)
    rims, wy = half // group, 2 * half
    begin = (hz - rad) * (1 - zh)
    lane = lane_of((width, hz)) // rad
    for o in range(2 * rims):
        total = None
        for m in range(group):
            value = pltpu.roll(row_of(a, b, o * group + m, half), (rad * m - begin + hz) % hz, 1)
            total = value if m == 0 else jnp.where(lane == m, value, total)
        edge[o] = total
        to_z[2 * rims + o] = total
        to_z[o] = (a if o < rims else b)[half + o % rims]
    hy = wy - rad
    over = hy // group
    for y in range(wy):
        @pl.when(jnp.logical_and(y >= rad * (1 - yh), y < rad * (1 - yh) + hy))
        def _():
            to_y[y - rad * (1 - yh)] = row_of(a, b, y, half)
    skip = (rad // group) * (1 - yh)
    for k in range(over):
        to_y[hy + k] = to_z[skip + k]
        to_c[k] = to_z[skip + k]
        to_c[over + k] = edge[skip + k]


def update_kernel(rad, place, a, b, fy, fz, fc, old_a, old_b, count, new_a, new_b):
    yh, zh = place[0], place[1]
    rows, width, hz = a.shape
    group = hz // rad
    half = rows * group // (group + 1)
    rims, wy = half // group, 2 * half
    hy = wy - rad
    over = hy // group
    start, skip = rad * (1 - yh), (rad // group) * (1 - yh)
    begin = (hz - rad) * (1 - zh)
    zero = jnp.zeros((width, hz), F32)
    inside = (lane_of((width, hz)) >= begin) & (lane_of((width, hz)) < begin + rad)
    total = count[...]

    def part(ref, first, at, limit):
        ok = jnp.logical_and(at >= 0, at < limit)
        return jnp.where(ok, ref[first + jnp.clip(at, 0, limit - 1)], zero)

    for o in range(2 * rims):
        h, k = o // rims, o % rims
        old, new, row = (old_a, old_b)[h], (new_a, new_b)[h], half + k
        rim = (a, b)[h][half + k] + fz[2 * rims + o]
        rim = rim + part(fy, hy, o - skip, over) + part(fc, over, o - skip, over)
        new[row] = old[row] * rim / total
        edge = fz[o] + part(fc, 0, o - skip, over)
        for m in range(group):
            y = o * group + m
            moved = jnp.where(inside, pltpu.roll(edge, (begin - rad * m + hz) % hz, 1), 0.0)
            value = row_of(a, b, y, half) + part(fy, 0, y - start, hy) + moved
            row = y - h * half
            new[row] = old[row] * value / total


def last_pack_kernel(rad, place, a, b, to_y, to_z, to_c):
    rows, _, hz = a.shape
    group = hz // rad
    half = rows * group // (group + 1)
    rims, own = half // group, 2 * half - rad
    for side in range(2):

        @pl.when(place[0] == side)
        def _():
            outer = own * (1 - side)
            for k in range(rad):
                to_y[k] = row_of(a, b, outer + k, half)
            for ref, first in ((to_z, rad * side // group), (to_c, outer // group)):
                for k in range(ref.shape[0]):
                    o = first + k
                    ref[k] = (a if o < rims else b)[half + o % rims]


def last_update_kernel(rad, place, a, b, fy, fz, fc, old_a, old_b, count, new):
    rows, width, hz = a.shape
    group = hz // rad
    half = rows * group // (group + 1)
    own = new.shape[1]
    begin = (hz - rad) * (1 - place[1])
    inside = (lane_of((width, hz)) >= begin) & (lane_of((width, hz)) < begin + rad)
    total = count[...]
    for side in range(2):

        @pl.when(place[0] == side)
        def _():
            first = (own - rad) * (1 - side)
            for k in range(own):
                y = rad * side + k
                value, edge = row_of(a, b, y, half), fz[k // group]
                if first <= k < first + rad:
                    value = value + fy[k - first]
                    edge = edge + fc[(k - first) // group]
                moved = pltpu.roll(edge, (begin - rad * (k % group) + hz) % hz, 1)
                value = value + jnp.where(inside, moved, 0.0)
                new[:, k, :] = row_of(old_a, old_b, y, half) * value / total


def assemble_kernel(where, *refs):
    pieces, out = refs[:-1], refs[-1]
    _, hy, hz = pieces[0].shape
    for r, piece in enumerate(pieces):
        for owner in range(len(pieces)):
            oz, oy = owner >> 1, (owner ^ (owner >> 1)) & 1

            @pl.when(where[0] == owner ^ r)
            def _():
                out[:, oy * hy : (oy + 1) * hy, oz * hz : (oz + 1) * hz] = piece[...]


VMEM = pl.BlockSpec(memory_space=pltpu.VMEM)
ANY = pl.BlockSpec(memory_space=pl.ANY)
SMEM = pl.BlockSpec(memory_space=pltpu.SMEM)


def call(kernel, shapes, scratch, smem, cost, *args, late=()):
    flops, moved = cost
    return pl.pallas_call(
        kernel,
        out_shape=[jax.ShapeDtypeStruct(shape, F32) for shape in shapes],
        in_specs=[SMEM] * smem + [VMEM] * (len(args) - smem) + [ANY] * len(late),
        out_specs=[VMEM] * len(shapes),
        scratch_shapes=[pltpu.VMEM(s, F32) if isinstance(s, tuple) else s for s in scratch],
        compiler_params=PARAMS,
        cost_estimate=pl.CostEstimate(flops=flops, bytes_accessed=moved, transcendentals=0),
    )(*args, *late)


def body(prior, data, taps, offsets, coverage):
    nview, nspace = lax.axis_size("view"), lax.axis_size("space")
    g, j = lax.axis_index("view"), lax.axis_index("space")
    zh, yh = g >> 1, (g ^ (g >> 1)) & 1
    place_yz = jnp.stack([yh, zh, j]).astype(jnp.int32)
    local, width, ny, nz = data.shape
    ntaps = taps.shape[-1]
    rad = ntaps // 2
    hy, hz = ny // 2, nz // 2
    wy = hy + rad
    group = hz // rad
    half, rims = wy // 2, wy // 2 // group
    rows = half + rims

    flat = jnp.concatenate(
        [
            taps.reshape(local, -1),
            offsets.astype(jnp.float32)[:, None],
            coverage.astype(jnp.float32),
        ],
        axis=1,
    )
    used = flat.shape[1]
    flat = jnp.pad(flat, ((0, 0), (0, -used % LANES)))
    shared = [flat] + [swap(flat, "view", r) for r in range(1, nview)]
    shared = jnp.concatenate(shared, axis=0)

    def quadrant(owner):
        oz, oy = owner >> 1, (owner ^ (owner >> 1)) & 1
        return lax.dynamic_slice(data, (0, 0, oy * hy, oz * hz), (local, width, hy, hz))

    pieces = [quadrant(g)] + [swap(quadrant(g ^ r), "view", r) for r in range(1, nview)]

    nviews = nview * local
    nvi = nviews * width
    kern = shared[:, : 3 * ntaps].reshape(nviews, 3, ntaps)
    kern = kern / jnp.sum(kern, axis=-1, keepdims=True)
    turn = shared[:, 3 * ntaps].astype(jnp.int32)
    cover = shared[:, 3 * ntaps + 1 : used]
    count = jnp.broadcast_to(jnp.sum(cover, axis=0)[:, None], (width, hz))
    note = jnp.pad(cover.T, ((0, 0), (0, hz - nviews)))[None]

    window = lax.dynamic_slice_in_dim(prior, rad * yh, wy, axis=1).transpose(1, 0, 2)
    main = lax.dynamic_slice_in_dim(window, hz * zh, hz, axis=2)
    rim = lax.dynamic_slice_in_dim(window, jnp.where(zh == 0, hz, hz - rad), rad, axis=2)
    rim = rim.reshape(2 * rims, group, width, rad).transpose(0, 2, 1, 3).reshape(2 * rims, width, hz)
    parts = [main[:half], rim[:rims], main[half:], rim[rims:]]
    estimate = [jnp.concatenate(parts[:2], axis=0), jnp.concatenate(parts[2:], axis=0)]
    wide = gather(estimate)
    notes = gather([note])

    nx = nspace * width
    wx, bxt, kz, kzt = pl.pallas_call(
        functools.partial(bands_kernel, rad),
        out_shape=[
            jax.ShapeDtypeStruct((nvi, 3 * nx), BF16),
            jax.ShapeDtypeStruct((nx, nvi), F32),
            jax.ShapeDtypeStruct((nviews, 4 * hz, hz), BF16),
            jax.ShapeDtypeStruct((nviews, 3 * hz, 2 * hz), BF16),
        ],
        in_specs=[SMEM] * 3,
        out_specs=[VMEM] * 4,
        compiler_params=PARAMS,
        cost_estimate=pl.CostEstimate(flops=nviews * hz * hz * 32, bytes_accessed=nviews * hz * hz * 16, transcendentals=0),
    )(place_yz, (j - turn) % nspace, kern.reshape(nviews, -1))
    ky = kern[:, 1]

    plane = width * hz
    mxu = 2 * 3 * nvi * plane * 2 * rows * (nspace // 2)

    def ahead(wide, late, cost):
        return call(
            functools.partial(ahead_kernel, rad),
            [(hy, nvi, hz)],
            [(wy, nvi, hz), pltpu.VMEM((wy, nvi, hz), BF16), (wy + rad, width, hz), (wy + rad, width, hz)],
            2,
            cost,
            place_yz, ky, wx, kz, *wide,
            late=late,
        )[0]

    def back(blurred):
        return call(
            functools.partial(back_kernel, rad, nview),
            [(nspace // 2, rows, width, hz)] * 4,
            [(hy, nvi, hz), (hy + 2 * rad, width, hz), (hy + 2 * rad, width, hz), (wy, nvi, hz), (2 * rims, nvi, hz), pltpu.VMEM((nx, 3 * nvi), BF16)],
            2,
            (mxu, 4 * plane * (nspace * 2 * rows + 2 * hy * nviews)),
            place_yz, ky, bxt, *notes, kzt, blurred, *pieces,
        )

    over = hy // group
    for step in range(ITERS):
        if step:
            wide = gather(estimate)
        blurred = ahead(wide, () if step else tuple(pieces[1:3]), (mxu if step else 0, plane))
        sums = back(blurred)
        a, b = scatter_sum(sums[:2], sums[2:])
        last = step == ITERS - 1
        if last:
            sizes, scratch = (rad, over, rad // group), []
            results = [(width, hy, hz)]
        else:
            sizes, scratch = (hy + over, 4 * rims, 2 * over), [(2 * rims, width, hz)]
            results = [(rows, width, hz)] * 2
        to_y, to_z, to_c = call(
            functools.partial(last_pack_kernel if last else pack_kernel, rad),
            [(size, width, hz) for size in sizes],
            scratch,
            1,
            (plane, 4 * plane * 4 * rows),
            place_yz, a, b,
        )
        estimate = call(
            functools.partial(last_update_kernel if last else update_kernel, rad),
            results,
            [],
            1,
            (plane, 4 * plane * 8 * rows),
            place_yz, a, b, swap(to_y, "view", 1), swap(to_z, "view", 3), swap(to_c, "view", 2), *estimate, count,
        )

    own = estimate[0]
    parts = [own] + [swap(own, "view", r) for r in range(1, nview)]
    return call(
        assemble_kernel,
        [(width, ny, nz)],
        [],
        1,
        (plane, 16 * plane * ny),
        g.astype(jnp.int32)[None], *parts,
    )[0]


def solution(mesh):
    return jax.shard_map(
        body,
        mesh=mesh,
        in_specs=(
            P("space", None, None),
            P("view", "space", None, None),
            P("view", None, None),
            P("view"),
            P("view", "space"),
        ),
        out_specs=P("space", None, None),
        check_vma=False,
    )
```
